32 devices in a mesh: blk: 8 (over z, y), rep: 4 (over x, core).
Axes of the slice: x: 2, y: 2, z: 4, core: 2. Of those that a mesh axis runs over, the one named last changes fastest.
Arguments:
- tiles: bfloat16 [8, 32, 128, 128], P('blk', 'rep'), may hold values from -6 to 6
- tile_rows: int32 [8, 32], P('blk', 'rep'), may hold values from 0 to 15
- tile_cols: int32 [8, 32], P('blk', 'rep'), may hold values from 0 to 63
- start_right: float32 [65536, 64], P(('blk', 'rep')), may hold values from -6 to 6
Outputs:
- left_vectors: float32 [16384, 64], P('blk')
- right_vectors: float32 [65536, 64], P(('blk', 'rep'))
The draws below stay inside these ranges and needn't reach their ends.
All inputs are finite; a program needn't handle non-finite values.
Results may differ from the reference program's by a relative error of at most 0.022.
Values may be sent and summed in bfloat16 or wider, within the bound.
No kernel may reach another device: no remote copies, remote signals or barrier semaphores. Data moves between devices by JAX's collectives and lax.ppermute only.
A program may use at most 64 MiB of HBM per device.

```python
import math
import jax
import jax.numpy as jnp
from jax import lax

TILE = 128
K = 64
ITERS = 2
COL_TILES = 64
ROW_TILES = 16
SLOTS = 1
TILES_DEV = 8
TILES_ROW = 32
COLUMN_TILES = 512
ROWS = 16384
COLS = 65536
N_BLK = 8


def set_ends(values, own_key, low, top_value):
    dims = values.shape
    index_at = [jax.random.randint(jax.random.fold_in(own_key, axis), (), 0, dims[axis]) for axis in range(len(dims))]
    values = values.at[tuple(index_at)].set(low)
    longest = dims.index(max(dims))
    index_at[longest] = (index_at[longest] + 1) % dims[longest]
    return values.at[tuple(index_at)].set(top_value)


def block_scale(stream_key, dims, pieces, smallest, top_value):
    gain, own = 1.0, jax.random.fold_in(stream_key, 6)
    for dim, parts in pieces:
        heights = jnp.exp(jax.random.uniform(jax.random.fold_in(own, dim), (parts,), jnp.float32, smallest / len(pieces), top_value / len(pieces)))
        gain = gain * jnp.repeat(heights, dims[dim] // parts).reshape([-1 if axis == dim else 1 for axis in range(len(dims))])
    return gain


def centred(stream_key, extent, deviation, bound, split=(), held_as=jnp.bfloat16):
    values = jax.random.normal(stream_key, extent, jnp.float32) * deviation
    if len(split) > 0:
        values = block_scale(stream_key, extent, split, -0.22, 0.18) * values
    return jnp.clip(values, min=-bound, max=bound).astype(held_as)


def setup_inputs(seed: int = 0) -> dict:
    key_list = jax.random.split(jax.random.key(seed), 5)
    return {
        "tiles": centred(key_list[0], (N_BLK, TILES_ROW, TILE, TILE), 1.0, 6.0, ((0, 8), (1, 4))),
        "tile_rows": set_ends(jax.random.randint(key_list[1], (N_BLK, TILES_ROW), 0, ROW_TILES), jax.random.fold_in(key_list[1], 1), 0, ROW_TILES - 1).astype(jnp.int32),
        "tile_cols": set_ends(jax.random.randint(key_list[2], (N_BLK, TILES_ROW), 0, COL_TILES), jax.random.fold_in(key_list[2], 1), 0, COL_TILES - 1).astype(jnp.int32),
        "start_right": centred(key_list[3], (COLS, K), 1.0, 6.0, ((0, 32),), jnp.float32),
    }


def normalize(matrix):
    gram_matrix = jnp.dot(matrix.T.astype(jnp.float32), matrix.astype(jnp.float32), precision=lax.Precision.HIGHEST, preferred_element_type=jnp.float32)
    factor = jnp.linalg.cholesky(gram_matrix)
    return jax.scipy.linalg.solve_triangular(factor, matrix.T, lower=True).T

def reference(tiles, tile_rows, tile_cols, start_right):
    owners = jnp.arange(TILES_ROW, dtype=jnp.int32) % TILES_DEV // SLOTS
    right = start_right
    left = jnp.zeros((ROWS, K), jnp.float32)
    for iteration in range(ITERS):
        right_narrow = right.astype(jnp.bfloat16).reshape(COLUMN_TILES, TILE, K)

        def left_block(inputs):
            block_tiles, block_rows, block_cols = inputs
            global_cols = (owners * COL_TILES + block_cols).astype(jnp.int32)
            chosen = right_narrow[global_cols].astype(jnp.float32)
            products = jnp.einsum('tab,tbk->tak', block_tiles.astype(jnp.float32), chosen, precision=lax.Precision.HIGHEST)
            summed = jnp.zeros((ROW_TILES, TILE, K), jnp.float32).at[block_rows].add(products)
            return summed.reshape(ROW_TILES * TILE, K)
        left_raw = lax.map(left_block, (tiles, tile_rows, tile_cols)).reshape(ROWS, K)
        left = normalize(left_raw)
        left_narrow = left.astype(jnp.bfloat16).reshape(N_BLK, ROW_TILES, TILE, K)

        def add_block(total, inputs):
            block_tiles, block_rows, block_cols, left_block_rows = inputs
            global_cols = (owners * COL_TILES + block_cols).astype(jnp.int32)
            chosen = left_block_rows[block_rows].astype(jnp.float32)
            products = jnp.einsum('tab,tak->tbk', block_tiles.astype(jnp.float32), chosen, precision=lax.Precision.HIGHEST)
            return (total.at[global_cols].add(products), None)
        start_total = jnp.zeros((COLUMN_TILES, TILE, K), jnp.float32)
        right_raw = lax.scan(add_block, start_total, (tiles, tile_rows, tile_cols, left_narrow))[0].reshape(COLS, K)
        right = normalize(right_raw)
    return (left * math.sqrt(ROWS), right * math.sqrt(COLS))
```

```python
import functools
import math

import jax
import jax.numpy as jnp
from jax import lax
from jax.experimental import pallas as pl
from jax.experimental.pallas import tpu as pltpu
from jax.sharding import PartitionSpec as P

ITERS = 2
ROW_TILES = 16
F32 = jnp.float32
BF16 = jnp.bfloat16
VMEM_BYTES = 48 * 1024 * 1024
NT = (((1,), (1,)), ((), ()))
NN = (((1,), (0,)), ((), ()))


def dot(a, b, dims):
    return lax.dot_general(a, b, dims, preferred_element_type=F32)


def split3(value):
    high = value.astype(BF16)
    rest = value - high.astype(F32)
    middle = rest.astype(BF16)
    low = (rest - middle.astype(F32)).astype(BF16)
    return high, middle, low


def gram_of(value):
    width = value.shape[0]
    high, middle, low = split3(value)
    parts = jnp.concatenate([high, middle, low], axis=0)
    full = dot(parts, parts, NT)

    def block(i, j):
        return full[i * width : (i + 1) * width, j * width : (j + 1) * width]

    small = block(1, 1) + block(0, 2) + block(2, 0)
    return block(0, 0) + (block(0, 1) + block(1, 0) + small)


def eliminate(work):
    size = work.shape[0]
    for k in range(size // 8):
        at = size + 8 * k
        panel = work[8 * k : 8 * k + 8, :]
        shape = panel.shape
        cols = [jnp.broadcast_to(panel[:, at + s : at + s + 1], shape) for s in range(8)]
        d = {(i, s): jnp.broadcast_to(cols[s][i : i + 1, :], shape) for s in range(8) for i in range(s, 8)}
        rows = [jnp.broadcast_to(panel[s : s + 1, :], shape) for s in range(8)]
        inverse = [None] * 8
        lower = {}
        for s in range(8):
            inverse[s] = 1.0 / d[s, s]
            for i in range(s + 1, 8):
                lower[i, s] = d[i, s] * inverse[s]
            for i in range(s + 1, 8):
                for j in range(s + 1, i + 1):
                    d[i, j] = d[i, j] - lower[i, s] * d[j, s]
                rows[i] = rows[i] - lower[i, s] * rows[s]
        solved = [None] * 8
        for s in reversed(range(8)):
            solved[s] = rows[s] * inverse[s]
            for i in range(s + 1, 8):
                solved[s] = solved[s] - lower[i, s] * solved[i]
        for i in range(k + 1, size // 8):
            rest = work[8 * i : 8 * i + 8, :]
            updated = rest
            for s in range(8):
                updated = updated - jnp.broadcast_to(rest[:, at + s : at + s + 1], shape) * solved[s]
            work[8 * i : 8 * i + 8, :] = updated
        for s in range(8):
            work[8 * k + s : 8 * k + s + 1, :] = (rows[s] * lax.rsqrt(d[s, s]))[0:1, :]


def put_identity(work):
    size = work.shape[0]
    row = lax.broadcasted_iota(jnp.int32, (size, size), 0)
    column = lax.broadcasted_iota(jnp.int32, (size, size), 1)
    work[:, 0:size] = jnp.where(row == column, 1.0, 0.0).astype(F32)


def pack_half_gram(gram_half):
    high, middle, low = split3(gram_half)
    half = gram_half.shape[0] // 2
    return jnp.concatenate(
        [
            jnp.concatenate([high, middle], axis=1),
            jnp.concatenate([low[0:half], low[half:]], axis=1),
        ],
        axis=0,
    )


def unpack_half_gram(ref, at, width):
    half = width // 2
    total = jnp.zeros((half, width), F32)
    top = jnp.zeros((half, 2 * width), F32)
    bottom = jnp.zeros((half // 2, 2 * width), F32)
    for b in range(ref.shape[0]):
        top = top + ref[b, at : at + half, :].astype(F32)
        bottom = bottom + ref[b, at + half : at + half + half // 2, :].astype(F32)
    total = top[:, 0:width] + top[:, width:]
    return total + jnp.concatenate([bottom[:, 0:width], bottom[:, width:]], axis=0)


def factor(work, own_ref, other_ref, core, at, width):
    half = width // 2
    put_identity(work)
    work[pl.ds(pl.multiple_of(core * half, half), half), width : 2 * width] = unpack_half_gram(own_ref, at, width)
    work[pl.ds(pl.multiple_of((1 - core) * half, half), half), width : 2 * width] = unpack_half_gram(
        other_ref, at, width
    )
    eliminate(work)
    return work[:, 0:width]


def normalise_tile(scale_parts, tile):
    width = tile.shape[0]
    both = dot(scale_parts, tile, NN)
    return (both[0:width] + both[width:]).astype(BF16)


def two_parts(scale):
    high = scale.astype(BF16)
    return jnp.concatenate([high, (scale - high.astype(F32)).astype(BF16)], axis=0)


def choose_kernel(cols_ref, place_ref, own_ref, near_ref, out_ref):
    rep = place_ref[0]
    core = lax.rem(rep, 2)
    tile = own_ref.shape[2] // place_share(own_ref)
    per_share = own_ref.shape[2] // tile
    blocks = out_ref.shape[0]
    width = own_ref.shape[1]
    for b in range(blocks):
        for x in range(2):
            col = cols_ref[b, x * 2 + core]
            share = lax.div(col, per_share)
            at = pl.multiple_of(lax.rem(col, per_share) * tile, tile)
            away = lax.bitwise_xor(share, rep)
            same_core = lax.rem(away, 2) == 0
            far = lax.div(away, 2)
            mine = own_ref[far, :, pl.ds(at, tile)]
            theirs = near_ref[far, :, pl.ds(at, tile)]
            out_ref[b, x * width : (x + 1) * width, :] = jnp.where(same_core, mine, theirs)


def place_share(ref):
    return ref.shape[2] // 128


def left_kernel(first, rows_ref, place_ref, tiles_ref, own_ref, other_ref, out_ref, raw_ref, work):
    core = lax.rem(place_ref[0], 2)
    pieces = own_ref.shape[0]
    width = raw_ref.shape[0]
    tile = tiles_ref.shape[-1]
    if not first:
        scale = two_parts(factor(work, own_ref, other_ref, core, 2 * width, width))
    raw_ref[...] = jnp.zeros_like(raw_ref)
    for source, at_core in ((own_ref, core), (other_ref, 1 - core)):
        for x in range(2):
            rep = x * 2 + at_core

            def add(p, source=source, x=x, rep=rep):
                chosen = source[p, x * width : (x + 1) * width, :]
                if not first:
                    chosen = normalise_tile(scale, chosen)
                product = dot(chosen, tiles_ref[rep, p], NT)
                at = pl.multiple_of(rows_ref[rep, p] * tile, tile)
                raw_ref[:, pl.ds(at, tile)] += product

            each(pieces, add)
    gram = gram_of(raw_ref[...])
    half = width // 2
    work[:, width : 2 * width] = gram
    packed = pack_half_gram(work[pl.ds(pl.multiple_of(core * half, half), half), width : 2 * width])

    def send(p):
        for x in range(2):
            at = pl.multiple_of(rows_ref[x * 2 + core, p] * tile, tile)
            out_ref[p, x * width : (x + 1) * width, :] = raw_ref[:, pl.ds(at, tile)].astype(BF16)
        out_ref[p, 2 * width :, :] = packed

    each(pieces, send)


def each(count, body):
    if count <= 8:
        for i in range(count):
            body(i)
    else:
        lax.fori_loop(0, count // 8, lambda o, c: [body(o * 8 + i) for i in range(8)] and c, 0)


def right_kernel(last, cols_ref, fresh_ref, place_ref, tiles_ref, own_ref, other_ref, out_ref, *rest):
    if last:
        share_ref, scale_ref, raw, stacked, work = rest
    else:
        raw, stacked, work = rest
    core = lax.rem(place_ref[0], 2)
    blocks = own_ref.shape[0]
    width = raw.shape[1]
    tile = raw.shape[2]
    full_scale = factor(work, own_ref, other_ref, core, 2 * width, width)
    if last:
        scale_ref[...] = full_scale
    scale = two_parts(full_scale)
    raw[...] = jnp.zeros_like(raw)
    for source, at_core in ((own_ref, core), (other_ref, 1 - core)):
        for x in range(2):
            rep = x * 2 + at_core

            def add(b, source=source, x=x, rep=rep):
                chosen = normalise_tile(scale, source[b, x * width : (x + 1) * width, :])
                raw[cols_ref[b, rep]] += dot(chosen, tiles_ref[rep, b, 0:tile, :], NN)

            each(blocks, add)
    gram = jnp.zeros((width, width), F32)
    half = width // 2

    def take(b, base):
        for rep in range(4):
            value = raw[cols_ref[b, rep]] * fresh_ref[b, rep].astype(F32)
            at = (b * 4 + rep - base) * tile
            if not isinstance(at, int):
                at = pl.multiple_of(at, tile)
            high, middle, low = split3(value)
            stacked[0:width, pl.ds(at, tile)] = high
            stacked[width : 2 * width, pl.ds(at, tile)] = middle
            stacked[2 * width :, pl.ds(at, tile)] = low

    def add_gram(base):
        for b in range(8):
            take(base + b, base * 4)
        parts = stacked[...]
        full = dot(parts, parts, NT)

        def block(i, j):
            return full[i * width : (i + 1) * width, j * width : (j + 1) * width]

        small = block(1, 1) + block(0, 2) + block(2, 0)
        return block(0, 0) + (block(0, 1) + block(1, 0) + small)

    if blocks == 8:
        gram = add_gram(0)
    else:
        gram = lax.fori_loop(0, blocks // 8, lambda o, g: g + add_gram(o * 8), gram)
    if last:
        both = jnp.concatenate([gram[0:half], gram[half:]], axis=1)

        def send(b):
            out_ref[b] = both

        each(blocks, send)
        shares = share_ref.shape[1] // tile
        for i in range(shares):
            share_ref[:, i * tile : (i + 1) * tile] = raw[place_ref[0] * shares + i]
        return
    work[:, width : 2 * width] = gram
    packed = pack_half_gram(work[pl.ds(pl.multiple_of(core * half, half), half), width : 2 * width])

    def send(b):
        for x in range(2):
            out_ref[b, x * width : (x + 1) * width, :] = raw[cols_ref[b, x * 2 + core]].astype(BF16)
        out_ref[b, 2 * width :, :] = packed

    each(blocks, send)


def finish_kernel(left_factor, right_factor, gram_ref, scale_ref, left_ref, share_ref, left_out, right_out, work):
    width = left_ref.shape[0]
    half = width // 2
    total = gram_ref[0]
    for b in range(1, gram_ref.shape[0]):
        total = total + gram_ref[b]
    put_identity(work)
    work[0:half, width : 2 * width] = total[:, 0:width]
    work[half:, width : 2 * width] = total[:, width:]
    eliminate(work)
    right_out[...] = lax.dot_general(
        work[:, 0:width] * right_factor,
        share_ref[...],
        NN,
        precision=lax.Precision.HIGHEST,
        preferred_element_type=F32,
    )
    left_out[...] = lax.dot_general(
        scale_ref[...] * left_factor,
        left_ref[...],
        NN,
        precision=lax.Precision.HIGHEST,
        preferred_element_type=F32,
    )


SMEM = pl.BlockSpec(memory_space=pltpu.SMEM)
VMEM = pl.BlockSpec(memory_space=pltpu.VMEM)


def call(kernel, outs, smem, vmem, scratch=()):
    return pl.pallas_call(
        kernel,
        out_shape=outs,
        in_specs=[SMEM] * len(smem) + [VMEM] * len(vmem),
        out_specs=[VMEM] * len(outs),
        scratch_shapes=list(scratch),
        compiler_params=pltpu.CompilerParams(vmem_limit_bytes=VMEM_BYTES),
    )(*smem, *vmem)


def local(tiles, tile_rows, tile_cols, start_right):
    blocks = lax.axis_size("blk")
    group = lax.axis_size("rep")
    rep = lax.axis_index("rep").astype(jnp.int32)
    tile = tiles.shape[-1]
    share, width = start_right.shape
    flat_tiles = tiles.reshape(-1, tile, tile)
    total_rows = ROW_TILES * tile * blocks
    piece_tiles = share * group // tile
    total_cols = share * group * blocks
    place = rep.reshape(1)
    packed_rows = 2 * width + 3 * width // 4

    def across(value):
        return lax.all_to_all(value, "blk", split_axis=0, concat_axis=0, tiled=True)

    def swap_core(value):
        return lax.ppermute(value, "rep", [(i, i ^ 1) for i in range(group)])

    def swap_x(value):
        return lax.ppermute(value, "rep", [(i, i ^ 2) for i in range(group)])

    shape = jax.ShapeDtypeStruct
    work = pltpu.VMEM((width, 2 * width), F32)

    places = lax.all_gather(jnp.concatenate([tile_rows, tile_cols], axis=1).reshape(2, -1), "rep", axis=0)
    rows_all = places[:, 0, :]
    cols_all = places[:, 1, :]
    start = start_right.T.astype(BF16)
    start_own = jnp.stack([start, swap_x(start)])
    start_near = swap_core(start_own)
    row_tiles = lax.all_gather(flat_tiles, "rep", axis=0)

    asked = jnp.zeros((blocks, 16, tile), BF16).at[:, 0, 0:group].set(cols_all.T.astype(BF16))
    moved = across(jnp.concatenate([flat_tiles, asked], axis=1))
    cols_here = moved[:, tile, 0:group].astype(jnp.int32)
    column_tiles = lax.all_gather(moved, "rep", axis=0)
    flat_cols = cols_here.reshape(-1)
    count = flat_cols.shape[0]
    earlier = jnp.arange(count)[None, :] < jnp.arange(count)[:, None]
    seen = jnp.any((flat_cols[None, :] == flat_cols[:, None]) & earlier, axis=1)
    fresh = jnp.where(seen, 0, 1).astype(jnp.int32).reshape(blocks, group)

    (chosen,) = call(
        choose_kernel,
        [shape((blocks, 2 * width, tile), BF16)],
        [cols_here, place],
        [start_own, start_near],
    )
    for iteration in range(ITERS):
        first, last = iteration == 0, iteration == ITERS - 1
        chosen = across(chosen)
        picked, left_raw = call(
            functools.partial(left_kernel, first),
            [shape((blocks, packed_rows, tile), BF16), shape((width, ROW_TILES * tile), F32)],
            [rows_all, place],
            [row_tiles, chosen, swap_core(chosen)],
            [work],
        )
        picked = across(picked)
        outs = [shape((blocks, packed_rows, tile), BF16)]
        if last:
            outs = [
                shape((blocks, width // 2, 2 * width), F32),
                shape((width, share), F32),
                shape((width, width), F32),
            ]
        results = call(
            functools.partial(right_kernel, last),
            outs,
            [cols_here, fresh, place],
            [column_tiles, picked, swap_core(picked)],
            [
                pltpu.VMEM((piece_tiles, width, tile), F32),
                pltpu.VMEM((3 * width, 8 * group * tile), BF16),
                work,
            ],
        )
        chosen = results[0]
    gram, right_raw, left_scale = results
    left, right = call(
        functools.partial(finish_kernel, math.sqrt(total_rows), math.sqrt(total_cols)),
        [shape(left_raw.shape, F32), shape(right_raw.shape, F32)],
        [],
        [across(gram), left_scale, left_raw, right_raw],
        [work],
    )
    return (left.T, right.T)


def solution(mesh):
    in_specs = (
        P("blk", "rep", None, None),
        P("blk", "rep"),
        P("blk", "rep"),
        P(("blk", "rep"), None),
    )
    out_specs = (P("blk", None), P(("blk", "rep"), None))
    return jax.shard_map(local, mesh=mesh, in_specs=in_specs, out_specs=out_specs, check_vma=False)
```

```python
import functools
import math

import jax
import jax.numpy as jnp
from jax import lax
from jax.experimental import pallas as pl
from jax.experimental.pallas import tpu as pltpu
from jax.sharding import PartitionSpec as P

ITERS = 2
ROW_TILES = 16
F32 = jnp.float32
BF16 = jnp.bfloat16
VMEM_BYTES = 48 * 1024 * 1024
NT = (((1,), (1,)), ((), ()))
NN = (((1,), (0,)), ((), ()))


def dot(a, b, dims):
    return lax.dot_general(a, b, dims, preferred_element_type=F32)


def exact_dot(a, b):
    return lax.dot_general(a, b, NN, precision=lax.Precision.HIGHEST, preferred_element_type=F32)


def two_parts(value):
    high = value.astype(BF16)
    return high, (value - high.astype(F32)).astype(BF16)


def eliminate(work):
    size = work.shape[0]
    for k in range(size // 8):
        at = size + 8 * k
        panel = work[8 * k : 8 * k + 8, :]
        shape = panel.shape
        cols = [jnp.broadcast_to(panel[:, at + s : at + s + 1], shape) for s in range(8)]
        d = {(i, s): jnp.broadcast_to(cols[s][i : i + 1, :], shape) for s in range(8) for i in range(s, 8)}
        rows = [jnp.broadcast_to(panel[s : s + 1, :], shape) for s in range(8)]
        inverse = [None] * 8
        lower = {}
        for s in range(8):
            inverse[s] = 1.0 / d[s, s]
            for i in range(s + 1, 8):
                lower[i, s] = d[i, s] * inverse[s]
            for i in range(s + 1, 8):
                for j in range(s + 1, i + 1):
                    d[i, j] = d[i, j] - lower[i, s] * d[j, s]
                rows[i] = rows[i] - lower[i, s] * rows[s]
        solved = [None] * 8
        for s in reversed(range(8)):
            solved[s] = rows[s] * inverse[s]
            for i in range(s + 1, 8):
                solved[s] = solved[s] - lower[i, s] * solved[i]
        for i in range(k + 1, size // 8):
            rest = work[8 * i : 8 * i + 8, :]
            updated = rest
            for s in range(8):
                updated = updated - jnp.broadcast_to(rest[:, at + s : at + s + 1], shape) * solved[s]
            work[8 * i : 8 * i + 8, :] = updated
        for s in range(8):
            work[8 * k + s : 8 * k + s + 1, :] = (rows[s] * lax.rsqrt(d[s, s]))[0:1, :]
        yield


def run(steps):
    for _ in steps:
        pass


def put_identity(work):
    size = work.shape[0]
    row = lax.broadcasted_iota(jnp.int32, work.shape, 0)
    column = lax.broadcasted_iota(jnp.int32, work.shape, 1)
    work[...] = jnp.where(row == column, 1.0, 0.0).astype(F32)


def gather_gram(work, own_ref, other_ref, core):
    size = work.shape[0]
    half = size // 2
    put_identity(work)
    for source, at_core in ((own_ref, core), (other_ref, 1 - core)):
        total = jnp.zeros((half, 2 * size), F32)
        for b in range(source.shape[0]):
            total = total + source[b, 2 * size :, :].astype(F32)
        total = total + pltpu.roll(total, size, 1)
        at = pl.multiple_of(at_core * half, half)
        work[pl.ds(at, half), size:] = total[:, size:]


def gram_of_parts(parts):
    width = parts.shape[0] // 2
    full = dot(parts, parts, NT)
    full = full[0:width] + full[width:]
    return full + pltpu.roll(full, width, 1)


def apply_scale(scale_parts, value):
    high, low = two_parts(value)
    scale_high, scale_low = scale_parts
    return dot(
        jnp.concatenate([scale_high, scale_high, scale_low], axis=1),
        jnp.concatenate([high, low, high], axis=0),
        NN,
    )


def each(count, body, step=8):
    if count <= step:
        for i in range(count):
            body(i)
    else:

        def several(o, carry):
            for i in range(step):
                body(o * step + i)
            return carry

        lax.fori_loop(0, count // step, several, 0)


def beside(steps, tasks, count):
    if count > 8:
        run(steps)
        for task in tasks:
            each(count, task)
        return
    tasks = [functools.partial(task, i) for task in tasks for i in range(count)]
    panels = 8
    for n in range(panels):
        next(steps, None)
        for task in tasks[len(tasks) * n // panels : len(tasks) * (n + 1) // panels]:
            task()
    run(steps)


def choose_kernel(cols_ref, place_ref, own_ref, near_ref, out_ref):
    rep = place_ref[0]
    core = lax.rem(rep, 2)
    tile = out_ref.shape[2]
    per_share = own_ref.shape[2] // tile
    width = own_ref.shape[1]

    def choose(b):
        for x in range(2):
            col = cols_ref[b, x * 2 + core]
            share = lax.div(col, per_share)
            at = pl.multiple_of(lax.rem(col, per_share) * tile, tile)
            away = lax.bitwise_xor(share, rep)
            same_core = lax.rem(away, 2) == 0
            far = lax.div(away, 2)
            mine = own_ref[far, :, pl.ds(at, tile)]
            theirs = near_ref[far, :, pl.ds(at, tile)]
            out_ref[b, x * width : (x + 1) * width, :] = jnp.where(same_core, mine, theirs)

    each(out_ref.shape[0], choose)


def left_kernel(first, last, rows_ref, place_ref, tiles_hbm, own_ref, other_ref, out_ref, *rest):
    if last:
        raw_ref, *rest = rest
    total, stacked, packed, work, tiles, sems = rest
    core = lax.rem(place_ref[0], 2)
    pieces, _, tile = own_ref.shape
    width = total.shape[0]
    half = width // 2
    copies = [pltpu.make_async_copy(tiles_hbm.at[r], tiles.at[r], sems.at[r]) for r in range(4)]
    for copy in copies:
        copy.start()
    if not first:
        gather_gram(work, own_ref, other_ref, core)
    steps = eliminate(work) if not first else iter(())
    total[...] = jnp.zeros_like(total)

    tasks = []
    for x in range(2):
        for source, at_core in ((own_ref, core), (other_ref, 1 - core)):

            def add(p, source=source, x=x, rep=x * 2 + at_core):
                product = dot(source[p, x * width : (x + 1) * width, :], tiles[rep, p], NT)
                at = pl.multiple_of(rows_ref[rep, p] * tile, tile)
                total[:, pl.ds(at, tile)] += product

            tasks.append(add)
    next(steps, None)
    for copy in copies:
        copy.wait()
    beside(steps, tasks, pieces)
    value = total[...]
    if not first:
        value = apply_scale(two_parts(work[:, 0:width]), value)
    if last:
        raw_ref[...] = value
    high, low = two_parts(value)
    stacked[0:width, :] = high
    stacked[width:, :] = low
    pack_gram(gram_of_parts(stacked[...]), packed)
    mine = packed[pl.ds(pl.multiple_of(core * half, half), half), :]

    def send(p):
        for x in range(2):
            at = pl.multiple_of(rows_ref[x * 2 + core, p] * tile, tile)
            out_ref[p, x * width : (x + 1) * width, :] = stacked[0:width, pl.ds(at, tile)]
        out_ref[p, 2 * width :, :] = mine

    each(pieces, send)


def pack_gram(gram_twice, packed):
    high, low = two_parts(gram_twice)
    lane = lax.broadcasted_iota(jnp.int32, gram_twice.shape, 1)
    packed[...] = jnp.where(lane < gram_twice.shape[0], high.astype(F32), low.astype(F32)).astype(BF16)


def right_kernel(last, slots_ref, cols_ref, place_ref, tiles_hbm, own_ref, other_ref, out_ref, *rest):
    if last:
        share_ref, scale_ref, *rest = rest
    total, stacked, packed, work, tiles, sems = rest
    core = lax.rem(place_ref[0], 2)
    blocks, _, tile = own_ref.shape
    width = total.shape[0]
    half = width // 2
    quarter = tile // 4
    copies = [
        pltpu.make_async_copy(
            tiles_hbm.at[q, :, pl.ds(0, quarter), :], tiles.at[:, pl.ds(q * quarter, quarter), :], sems.at[q]
        )
        for q in range(4)
    ]
    for copy in copies:
        copy.start()
    gather_gram(work, own_ref, other_ref, core)
    steps = eliminate(work)
    total[...] = jnp.zeros_like(total)

    tasks = []
    for x in range(2):
        for source, at_core in ((own_ref, core), (other_ref, 1 - core)):

            def add(b, source=source, x=x, rep=x * 2 + at_core):
                product = dot(source[b, x * width : (x + 1) * width, :], tiles[b * 4 + rep], NN)
                at = pl.multiple_of(slots_ref[b, rep] * tile, tile)
                total[:, pl.ds(at, tile)] += product

            tasks.append(add)
    next(steps, None)
    for copy in copies:
        copy.wait()
    beside(steps, tasks, blocks)
    scale = work[:, 0:width]
    scale_parts = two_parts(scale)
    chunk = 8 * tile

    def apply(o):
        at = o * chunk if isinstance(o, int) else pl.multiple_of(o * chunk, chunk)
        high, low = two_parts(apply_scale(scale_parts, total[:, pl.ds(at, chunk)]))
        stacked[0:width, pl.ds(at, chunk)] = high
        stacked[width:, pl.ds(at, chunk)] = low

    each(total.shape[1] // chunk, apply)
    gram = gram_of_parts(stacked[...])
    if last:
        scale_ref[...] = scale
        both = jnp.concatenate([gram[0:half, 0:width], gram[half:, 0:width]], axis=1)

        def send(b):
            out_ref[b] = both

        each(blocks, send)
        shares = share_ref.shape[1] // tile
        share_ref[...] = jnp.zeros_like(share_ref)

        def keep(b):
            for rep in range(4):
                col = cols_ref[b, rep]

                @pl.when(lax.div(col, shares) == place_ref[0])
                def _():
                    to = pl.multiple_of(lax.rem(col, shares) * tile, tile)
                    at = pl.multiple_of(slots_ref[b, rep] * tile, tile)
                    share_ref[:, pl.ds(to, tile)] = total[:, pl.ds(at, tile)]

        each(blocks, keep)
        return
    pack_gram(gram, packed)
    mine = packed[pl.ds(pl.multiple_of(core * half, half), half), :]

    def send(b):
        for x in range(2):
            at = pl.multiple_of(slots_ref[b, x * 2 + core] * tile, tile)
            out_ref[b, x * width : (x + 1) * width, :] = stacked[0:width, pl.ds(at, tile)]
        out_ref[b, 2 * width :, :] = mine

    each(blocks, send)


def finish_left(factor, scale_ref, left_ref, left_out):
    left_out[...] = exact_dot(scale_ref[...] * factor, left_ref[...])


def finish_right(factor, gram_ref, scale_ref, share_ref, right_out, work):
    width = share_ref.shape[0]
    half = width // 2
    total = gram_ref[0]
    for b in range(1, gram_ref.shape[0]):
        total = total + gram_ref[b]
    put_identity(work)
    work[0:half, width:] = total[:, 0:width]
    work[half:, width:] = total[:, width:]
    run(eliminate(work))
    right_out[...] = exact_dot(exact_dot(work[:, 0:width], scale_ref[...]) * factor, share_ref[...])


SMEM = pl.BlockSpec(memory_space=pltpu.SMEM)
VMEM = pl.BlockSpec(memory_space=pltpu.VMEM)
ANY = pl.BlockSpec(memory_space=pl.ANY)


def call(kernel, outs, smem, held, vmem, scratch=()):
    return pl.pallas_call(
        kernel,
        out_shape=outs,
        in_specs=[SMEM] * len(smem) + [ANY] * len(held) + [VMEM] * len(vmem),
        out_specs=[VMEM] * len(outs),
        scratch_shapes=list(scratch),
        compiler_params=pltpu.CompilerParams(vmem_limit_bytes=VMEM_BYTES),
    )(*smem, *held, *vmem)


def local(tiles, tile_rows, tile_cols, start_right):
    blocks = lax.axis_size("blk")
    group = lax.axis_size("rep")
    block = lax.axis_index("blk")
    rep = lax.axis_index("rep").astype(jnp.int32)
    tile = tiles.shape[-1]
    share, width = start_right.shape
    flat_tiles = tiles.reshape(-1, tile, tile)
    held = flat_tiles.shape[0]
    quarter = tile // group
    total_rows = ROW_TILES * tile * blocks
    total_cols = share * group * blocks
    count = blocks * group
    place = rep.reshape(1)
    packed_rows = 2 * width + width // 2
    shape = jax.ShapeDtypeStruct

    def across(value):
        return lax.all_to_all(value, "blk", split_axis=0, concat_axis=0, tiled=True)

    def swap_core(value):
        return lax.ppermute(value, "rep", [(i, i ^ 1) for i in range(group)])

    def swap_x(value):
        return lax.ppermute(value, "rep", [(i, i ^ 2) for i in range(group)])

    start = start_right.T.astype(BF16)
    start_own = jnp.stack([start, swap_x(start)])
    start_near = swap_core(start_own)
    row_tiles = lax.all_gather(flat_tiles, "rep", axis=0)

    places = jnp.concatenate([tile_rows, tile_cols], axis=1).astype(BF16)
    places = jnp.pad(places, ((0, 7), (0, tile - 2 * held)))
    moved = jnp.concatenate(
        [flat_tiles.reshape(count, quarter, tile), jnp.broadcast_to(places, (count, 8, tile))], axis=1
    )
    moved = lax.all_to_all(moved, ("blk", "rep"), split_axis=0, concat_axis=0, tiled=True)
    places = moved[:, quarter, 0 : 2 * held].reshape(blocks, group, 2 * held).astype(jnp.int32)
    rows_all = lax.dynamic_index_in_dim(places, block, 0, keepdims=False)[:, 0:held]
    cols_here = lax.dynamic_index_in_dim(places, held + block, 2, keepdims=False)
    column_tiles = lax.all_gather(moved, "rep", axis=0)
    flat_cols = cols_here.reshape(-1)
    slots = jnp.argmax(flat_cols[:, None] == flat_cols[None, :], axis=1).astype(jnp.int32).reshape(blocks, group)

    (chosen,) = call(
        choose_kernel,
        [shape((blocks, 2 * width, tile), BF16)],
        [cols_here, place],
        [],
        [start_own, start_near],
    )
    packed = pltpu.VMEM((width, 2 * width), BF16)
    work = pltpu.VMEM((width, 2 * width), F32)
    sems = pltpu.SemaphoreType.DMA((4,))
    for iteration in range(ITERS):
        first, last = iteration == 0, iteration == ITERS - 1
        chosen = across(chosen)
        outs = [shape((blocks, packed_rows, tile), BF16)]
        if last:
            outs.append(shape((width, ROW_TILES * tile), F32))
        results = call(
            functools.partial(left_kernel, first, last),
            outs,
            [rows_all, place],
            [row_tiles],
            [chosen, swap_core(chosen)],
            [
                pltpu.VMEM((width, ROW_TILES * tile), F32),
                pltpu.VMEM((2 * width, ROW_TILES * tile), BF16),
                packed,
                work,
                pltpu.VMEM(row_tiles.shape, BF16),
                sems,
            ],
        )
        picked = across(results[0])
        left_raw = results[-1]
        outs = [shape((blocks, packed_rows, tile), BF16)]
        if last:
            outs = [
                shape((blocks, width // 2, 2 * width), F32),
                shape((width, share), F32),
                shape((width, width), F32),
            ]
        results = call(
            functools.partial(right_kernel, last),
            outs,
            [slots, cols_here, place],
            [column_tiles],
            [picked, swap_core(picked)],
            [
                pltpu.VMEM((width, count * tile), F32),
                pltpu.VMEM((2 * width, count * tile), BF16),
                packed,
                work,
                pltpu.VMEM((count, tile, tile), BF16),
                sems,
            ],
        )
        chosen = results[0]
    gram, right_raw, left_scale = results
    (left,) = call(
        functools.partial(finish_left, math.sqrt(total_rows)),
        [shape(left_raw.shape, F32)],
        [],
        [],
        [left_scale, left_raw],
    )
    (right,) = call(
        functools.partial(finish_right, math.sqrt(total_cols)),
        [shape(right_raw.shape, F32)],
        [],
        [],
        [across(gram), left_scale, right_raw],
        [work],
    )
    return (left.T, right.T)


def solution(mesh):
    in_specs = (
        P("blk", "rep", None, None),
        P("blk", "rep"),
        P("blk", "rep"),
        P(("blk", "rep"), None),
    )
    out_specs = (P("blk", None), P(("blk", "rep"), None))
    return jax.shard_map(local, mesh=mesh, in_specs=in_specs, out_specs=out_specs, check_vma=False)
```

```python
import functools
import math

import jax
import jax.numpy as jnp
from jax import lax
from jax.experimental import pallas as pl
from jax.experimental.pallas import tpu as pltpu
from jax.sharding import PartitionSpec as P

ITERS = 2
ROW_TILES = 16
F32 = jnp.float32
BF16 = jnp.bfloat16
VMEM_BYTES = 48 * 1024 * 1024
NT = (((1,), (1,)), ((), ()))
NN = (((1,), (0,)), ((), ()))


def dot(a, b, dims):
    return lax.dot_general(a, b, dims, preferred_element_type=F32)


def exact_dot(a, b):
    return lax.dot_general(a, b, NN, precision=lax.Precision.HIGHEST, preferred_element_type=F32)


def two_parts(value):
    high = value.astype(BF16)
    return high, (value - high.astype(F32)).astype(BF16)


def eliminate(work, spread):
    size = work.shape[0]
    for k in range(size // 8):
        at = size + 8 * k
        panel = work[8 * k : 8 * k + 8, :]
        shape = panel.shape
        for s in range(8):
            spread[k % 2, s] = jnp.broadcast_to(panel[:, at + s : at + s + 1], shape)
        d = {(i, s): jnp.broadcast_to(spread[k % 2, s, i : i + 1, :], shape) for s in range(8) for i in range(s, 8)}
        rows = [jnp.broadcast_to(work[8 * k + s : 8 * k + s + 1, :], shape) for s in range(8)]
        inverse = [None] * 8
        lower = {}
        for s in range(8):
            inverse[s] = 1.0 / d[s, s]
            for i in range(s + 1, 8):
                lower[i, s] = d[i, s] * inverse[s]
            for i in range(s + 1, 8):
                for j in range(s + 1, i + 1):
                    d[i, j] = d[i, j] - lower[i, s] * d[j, s]
                rows[i] = rows[i] - lower[i, s] * rows[s]
        for s in range(8):
            work[8 * k + s : 8 * k + s + 1, :] = (rows[s] * lax.rsqrt(d[s, s]))[0:1, :]
        solved = [rows[s] * inverse[s] for s in range(8)]
        below = [work[at : at + 8, :] for at in range(8 * k + 8, size, 8)]
        updated = list(below)
        for s in reversed(range(8)):
            for i in range(s):
                solved[i] = solved[i] - lower[s, i] * solved[s]
            for i, old in enumerate(below):
                updated[i] = updated[i] - jnp.broadcast_to(old[:, at + s : at + s + 1], shape) * solved[s]
        for i, new in enumerate(updated):
            work[8 * (k + 1 + i) : 8 * (k + 2 + i), :] = new
        yield


def run(steps):
    for _ in steps:
        pass


def put_identity(work):
    size = work.shape[0]
    row = lax.broadcasted_iota(jnp.int32, work.shape, 0)
    column = lax.broadcasted_iota(jnp.int32, work.shape, 1)
    work[...] = jnp.where(row == column, 1.0, 0.0).astype(F32)


def gather_gram(work, own_ref, other_ref, core):
    size = work.shape[0]
    half = size // 2
    put_identity(work)
    for source, at_core in ((own_ref, core), (other_ref, 1 - core)):
        total = jnp.zeros((half, 2 * size), F32)
        for b in range(source.shape[0]):
            total = total + source[b, 2 * size :, :].astype(F32)
        total = total + pltpu.roll(total, size, 1)
        at = pl.multiple_of(at_core * half, half)
        work[pl.ds(at, half), size:] = total[:, size:]


def gram_of_parts(parts):
    width = parts.shape[0] // 2
    full = dot(parts, parts, NT)
    full = full[0:width] + full[width:]
    return full + pltpu.roll(full, width, 1)


def apply_scale(scale_parts, value):
    high, low = two_parts(value)
    scale_high, scale_low = scale_parts
    return dot(
        jnp.concatenate([scale_high, scale_high, scale_low], axis=1),
        jnp.concatenate([high, low, high], axis=0),
        NN,
    )


def each(count, body, step=8):
    if count <= step:
        for i in range(count):
            body(i)
    else:

        def several(o, carry):
            for i in range(step):
                body(o * step + i)
            return carry

        lax.fori_loop(0, count // step, several, 0)


def beside(steps, tasks, count):
    if count > 8:
        run(steps)
        for task in tasks:
            each(count, task)
        return
    panels = 8
    done = 0
    for n in range(1, panels + 1):
        next(steps, None)
        while done < len(tasks) * count * n // panels:
            tasks[done // count](done % count)
            done += 1
    run(steps)


def pack_kernel(rows_hbm, cols_hbm, tiles_hbm, start_hbm, out_ref, start_out, rows_ref, cols_ref, tiles_ref, start_ref, sems):
    pairs = ((rows_hbm, rows_ref), (cols_hbm, cols_ref), (start_hbm, start_ref), (tiles_hbm, tiles_ref))
    copies = [pltpu.make_async_copy(source, to, sems.at[n]) for n, (source, to) in enumerate(pairs)]
    for copy in copies:
        copy.start()
    count, quarter, tile = tiles_ref.shape
    held = rows_ref.shape[1]
    lane = lax.broadcasted_iota(jnp.int32, (8, tile), 1)
    places = jnp.zeros((8, tile), jnp.int32)
    copies[0].wait()
    copies[1].wait()
    for j in range(held):
        places = jnp.where(lane == j, rows_ref[0, j], jnp.where(lane == held + j, cols_ref[0, j], places))
    places = places.astype(F32).astype(BF16)
    copies[2].wait()
    start_out[...] = start_ref[...].astype(BF16)
    copies[3].wait()

    def pack(i):
        out_ref[i] = jnp.concatenate([tiles_ref[i], places], axis=0)

    each(count, pack, 32)


def fetch_kernel(source, out_ref, sems):
    copies = [
        pltpu.make_async_copy(
            source.at[i, pl.ds(0, out_ref.shape[1]), pl.ds(0, out_ref.shape[2]), :], out_ref.at[i], sems.at[i]
        )
        for i in range(out_ref.shape[0])
    ]
    for copy in copies:
        copy.start()
    for copy in copies:
        copy.wait()


def choose_kernel(place_ref, moved_ref, own_ref, near_ref, out_ref, places_ref):
    rep, block = place_ref[0], place_ref[1]
    core = lax.rem(rep, 2)
    blocks, _, tile = out_ref.shape
    width, share = own_ref.shape[1:]
    per_share = share // tile
    lane = lax.broadcasted_iota(jnp.int32, (8, tile), 1)

    def choose(b):
        for r in range(4):
            entry = moved_ref[b * 4 + r]
            entry = entry[entry.shape[0] - 8 :, :].astype(F32)
            places_ref[b * 4 + r] = entry.astype(jnp.int32)
        for x in range(2):
            entry = moved_ref[b * 4 + x * 2 + core]
            entry = entry[entry.shape[0] - 8 :, :].astype(F32)
            col = jnp.max(jnp.where(lane == blocks + block, entry, 0.0)).astype(jnp.int32)
            at = pl.multiple_of(lax.rem(col, per_share) * tile, tile)
            away = lax.bitwise_xor(lax.div(col, per_share), rep)
            far = lax.div(away, 2)
            mine = own_ref[far, :, pl.ds(at, tile)]
            theirs = near_ref[far, :, pl.ds(at, tile)]
            out_ref[b, x * width : (x + 1) * width, :] = jnp.where(lax.rem(away, 2) == 0, mine, theirs)

    each(blocks, choose)


def find_slots(cols_ref, slots_ref, first_at):
    blocks, group = cols_ref.shape

    def note(o):
        b = blocks - 1 - o
        for r in reversed(range(group)):
            first_at[cols_ref[b, r]] = b * group + r

    def look(b):
        for r in range(group):
            slots_ref[b, r] = first_at[cols_ref[b, r]]

    each(blocks, note)
    each(blocks, look)


def left_kernel(first, last, rows_ref, place_ref, tiles_ref, own_ref, other_ref, out_ref, *rest):
    if last:
        raw_ref, *rest = rest
    total, stacked, packed, work, spread = rest
    core = lax.rem(place_ref[0], 2)
    pieces, _, tile = own_ref.shape
    width = total.shape[0]
    half = width // 2
    if not first:
        gather_gram(work, own_ref, other_ref, core)
    steps = eliminate(work, spread) if not first else iter(())
    total[...] = jnp.zeros_like(total)

    tasks = []
    for x in range(2):
        for source, at_core in ((own_ref, core), (other_ref, 1 - core)):

            def add(p, source=source, x=x, rep=x * 2 + at_core):
                product = dot(source[p, x * width : (x + 1) * width, :], tiles_ref[rep, p], NT)
                at = pl.multiple_of(rows_ref[rep, p] * tile, tile)
                total[:, pl.ds(at, tile)] += product

            tasks.append(add)
    beside(steps, tasks, pieces)
    value = total[...]
    if not first:
        value = apply_scale(two_parts(work[:, 0:width]), value)
    if last:
        raw_ref[...] = value
    high, low = two_parts(value)
    stacked[0:width, :] = high
    stacked[width:, :] = low
    pack_gram(gram_of_parts(stacked[...]), packed)
    mine = packed[pl.ds(pl.multiple_of(core * half, half), half), :]

    def send(p):
        for x in range(2):
            at = pl.multiple_of(rows_ref[x * 2 + core, p] * tile, tile)
            out_ref[p, x * width : (x + 1) * width, :] = stacked[0:width, pl.ds(at, tile)]
        out_ref[p, 2 * width :, :] = mine

    each(pieces, send)


def pack_gram(gram_twice, packed):
    high, low = two_parts(gram_twice)
    lane = lax.broadcasted_iota(jnp.int32, gram_twice.shape, 1)
    packed[...] = jnp.where(lane < gram_twice.shape[0], high.astype(F32), low.astype(F32)).astype(BF16)


def right_kernel(last, cols_ref, place_ref, tiles_ref, own_ref, other_ref, out_ref, *rest):
    if last:
        total, scale_ref, *rest = rest
    else:
        total, *rest = rest
    stacked, packed, work, spread, slots_ref, first_at = rest
    find_slots(cols_ref, slots_ref, first_at)
    core = lax.rem(place_ref[0], 2)
    blocks, _, tile = own_ref.shape
    width = total.shape[0]
    half = width // 2
    def stored(b, r):
        return jnp.concatenate([tiles_ref[q, b, r] for q in range(4)], axis=0)

    gather_gram(work, own_ref, other_ref, core)
    steps = eliminate(work, spread)
    total[...] = jnp.zeros_like(total)

    tasks = []
    for x in range(2):
        for source, at_core in ((own_ref, core), (other_ref, 1 - core)):

            def add(b, source=source, x=x, rep=x * 2 + at_core):
                product = dot(source[b, x * width : (x + 1) * width, :], stored(b, rep), NN)
                at = pl.multiple_of(slots_ref[b, rep] * tile, tile)
                total[:, pl.ds(at, tile)] += product

            tasks.append(add)
    beside(steps, tasks, blocks)
    scale = work[:, 0:width]
    scale_parts = two_parts(scale)
    chunk = 8 * tile

    def apply(o):
        at = o * chunk if isinstance(o, int) else pl.multiple_of(o * chunk, chunk)
        high, low = two_parts(apply_scale(scale_parts, total[:, pl.ds(at, chunk)]))
        stacked[0:width, pl.ds(at, chunk)] = high
        stacked[width:, pl.ds(at, chunk)] = low

    each(total.shape[1] // chunk, apply)
    gram = gram_of_parts(stacked[...])
    if last:
        scale_ref[...] = scale
        both = jnp.concatenate([gram[0:half, 0:width], gram[half:, 0:width]], axis=1)

        def send(b):
            out_ref[b] = both

        each(blocks, send)
        return
    pack_gram(gram, packed)
    mine = packed[pl.ds(pl.multiple_of(core * half, half), half), :]

    def send(b):
        for x in range(2):
            at = pl.multiple_of(slots_ref[b, x * 2 + core] * tile, tile)
            out_ref[b, x * width : (x + 1) * width, :] = stacked[0:width, pl.ds(at, tile)]
        out_ref[b, 2 * width :, :] = mine

    each(blocks, send)


def three_parts(value):
    high, low = two_parts(value)
    rest = value - high.astype(F32)
    return high, low, (rest - low.astype(F32)).astype(BF16)


def between_kernel(
    factor, cols_ref, place_ref, scale_ref, left_ref, total_ref, left_out, parts_ref, share, slots_ref, first_at
):
    width, tile = share.shape[0], total_ref.shape[1] // (slots_ref.shape[0] * 4)
    shares = share.shape[1] // tile
    find_slots(cols_ref, slots_ref, first_at)
    share[...] = jnp.zeros_like(share)

    def keep(b):
        for rep in range(4):
            col = cols_ref[b, rep]

            @pl.when(lax.div(col, shares) == place_ref[0])
            def _():
                to = pl.multiple_of(lax.rem(col, shares) * tile, tile)
                at = pl.multiple_of(slots_ref[b, rep] * tile, tile)
                share[:, pl.ds(to, tile)] = total_ref[:, pl.ds(at, tile)]

    each(slots_ref.shape[0], keep)
    high, middle, low = three_parts(share[...])
    for n, part in enumerate((high, middle, high, low, high, middle)):
        parts_ref[n * width : (n + 1) * width, :] = part
    left_out[...] = exact_dot(scale_ref[...] * factor, left_ref[...])


def finish_kernel(factor, gram_ref, scale_ref, parts_ref, right_hbm, work, spread, right, sems):
    width = scale_ref.shape[0]
    half = width // 2
    total = gram_ref[0]
    for b in range(1, gram_ref.shape[0]):
        total = total + gram_ref[b]
    put_identity(work)
    work[0:half, width:] = total[:, 0:width]
    work[half:, width:] = total[:, width:]
    run(eliminate(work, spread))
    high, middle, low = three_parts(exact_dot(work[:, 0:width], scale_ref[...]) * factor)
    scale = jnp.concatenate([high, high, middle, high, low, middle], axis=1)
    chunk = right.shape[1] // 4
    copies = []
    for n in range(4):
        at = pl.ds(n * chunk, chunk)
        right[:, at] = dot(scale, parts_ref[:, at], NN)
        copies.append(pltpu.make_async_copy(right.at[:, at], right_hbm.at[:, at], sems.at[n]))
        copies[-1].start()
    for copy in copies:
        copy.wait()


SMEM = pl.BlockSpec(memory_space=pltpu.SMEM)
VMEM = pl.BlockSpec(memory_space=pltpu.VMEM)
HBM = pl.BlockSpec(memory_space=pltpu.HBM)


def call(kernel, outs, smem, held, vmem, scratch=(), out_specs=None):
    return pl.pallas_call(
        kernel,
        out_shape=outs,
        in_specs=[SMEM] * len(smem) + [HBM] * len(held) + [VMEM] * len(vmem),
        out_specs=out_specs or [VMEM] * len(outs),
        scratch_shapes=list(scratch),
        compiler_params=pltpu.CompilerParams(vmem_limit_bytes=VMEM_BYTES),
    )(*smem, *[pltpu.with_memory_space_constraint(value, pltpu.HBM) for value in held], *vmem)


def local(tiles, tile_rows, tile_cols, start_right):
    blocks = lax.axis_size("blk")
    group = lax.axis_size("rep")
    block = lax.axis_index("blk")
    rep = lax.axis_index("rep").astype(jnp.int32)
    tile = tiles.shape[-1]
    share, width = start_right.shape
    flat_tiles = tiles.reshape(-1, tile, tile)
    held = flat_tiles.shape[0]
    quarter = tile // group
    total_rows = ROW_TILES * tile * blocks
    total_cols = share * group * blocks
    count = blocks * group
    place = jnp.stack([rep, block.astype(jnp.int32)])
    packed_rows = 2 * width + width // 2
    shape = jax.ShapeDtypeStruct

    def across(value):
        return lax.all_to_all(value, "blk", split_axis=0, concat_axis=0, tiled=True)

    def swap_x(value):
        return lax.ppermute(value, "rep", [(i, i ^ 2) for i in range(group)])

    def swap_core(value):
        return lax.ppermute(value, "rep", [(i, i ^ 1) for i in range(group)])

    moved, start = call(
        pack_kernel,
        [shape((count, quarter + 8, tile), BF16), shape((width, share), BF16)],
        [],
        [tile_rows, tile_cols, flat_tiles.reshape(count, quarter, tile), start_right.T],
        [],
        [
            pltpu.SMEM(tile_rows.shape, jnp.int32),
            pltpu.SMEM(tile_cols.shape, jnp.int32),
            pltpu.VMEM((count, quarter, tile), BF16),
            pltpu.VMEM((width, share), F32),
            pltpu.SemaphoreType.DMA((4,)),
        ],
    )
    start_own = jnp.stack([start, swap_x(start)])
    start_near = swap_core(start_own)
    flat_tiles, start = lax.optimization_barrier((flat_tiles, start))
    row_tiles = lax.all_gather(flat_tiles, "rep", axis=0)
    moved = lax.all_to_all(moved, ("blk", "rep"), split_axis=0, concat_axis=0, tiled=True)
    chosen, places = call(
        choose_kernel,
        [shape((blocks, 2 * width, tile), BF16), shape((count, 8, tile), jnp.int32)],
        [place],
        [],
        [moved, start_own, start_near],
    )
    places = places[:, 0, 0 : 2 * held].reshape(blocks, group, 2 * held)
    rows_all = lax.dynamic_index_in_dim(places, block, 0, keepdims=False)[:, 0:held]
    cols_here = lax.dynamic_index_in_dim(places, held + block, 2, keepdims=False)

    def fetch(value, rows):
        parts = value.shape[0]
        (value,) = call(
            fetch_kernel,
            [shape((*value.shape[:2], rows, value.shape[3]), BF16)],
            [],
            [value],
            [],
            [pltpu.SemaphoreType.DMA((parts,))],
        )
        return value

    packed = pltpu.VMEM((width, 2 * width), BF16)
    work = pltpu.VMEM((width, 2 * width), F32)
    spread = pltpu.VMEM((2, 8, 8, 2 * width), F32)
    slot_scratch = [pltpu.SMEM((blocks, group), jnp.int32), pltpu.SMEM((share * group // tile,), jnp.int32)]
    for iteration in range(ITERS):
        first, last = iteration == 0, iteration == ITERS - 1
        chosen = across(chosen)
        if first:
            chosen, moved, row_tiles = lax.optimization_barrier((chosen, moved, row_tiles))
            row_tiles = fetch(row_tiles.reshape(2 * group, -1, tile, tile), tile).reshape(row_tiles.shape)
            column_tiles = lax.all_gather(moved, "rep", axis=0)
        outs = [shape((blocks, packed_rows, tile), BF16)]
        if last:
            outs.append(shape((width, ROW_TILES * tile), F32))
        results = call(
            functools.partial(left_kernel, first, last),
            outs,
            [rows_all, place],
            [],
            [row_tiles, chosen, swap_core(chosen)],
            [
                pltpu.VMEM((width, ROW_TILES * tile), F32),
                pltpu.VMEM((2 * width, ROW_TILES * tile), BF16),
                packed,
                work,
                spread,
            ],
        )
        picked = across(results[0])
        left_raw = results[-1]
        if first:
            picked, column_tiles = lax.optimization_barrier((picked, column_tiles))
            column_tiles = column_tiles.reshape(2 * group, count // 2, -1, tile)
            column_tiles = fetch(column_tiles, quarter).reshape(group, blocks, group, quarter, tile)
        outs = [shape((blocks, packed_rows, tile), BF16)]
        if last:
            outs = [
                shape((blocks, width // 2, 2 * width), F32),
                shape((width, count * tile), F32),
                shape((width, width), F32),
            ]
        results = call(
            functools.partial(right_kernel, last),
            outs,
            [cols_here, place],
            [],
            [column_tiles, picked, swap_core(picked)],
            ([] if last else [pltpu.VMEM((width, count * tile), F32)])
            + [
                pltpu.VMEM((2 * width, count * tile), BF16),
                packed,
                work,
                spread,
            ]
            + slot_scratch,
        )
        chosen = results[0]
    gram, right_total, left_scale = results
    left, parts = call(
        functools.partial(between_kernel, math.sqrt(total_rows)),
        [shape(left_raw.shape, F32), shape((6 * width, share), BF16)],
        [cols_here, place],
        [],
        [left_scale, left_raw, right_total],
        [pltpu.VMEM((width, share), F32)] + slot_scratch,
    )
    (right,) = call(
        functools.partial(finish_kernel, math.sqrt(total_cols)),
        [shape((width, share), F32)],
        [],
        [],
        [across(gram), left_scale, parts],
        [work, spread, pltpu.VMEM((width, share), F32), pltpu.SemaphoreType.DMA((4,))],
        [HBM],
    )
    return (left.T, right.T)


def solution(mesh):
    in_specs = (
        P("blk", "rep", None, None),
        P("blk", "rep"),
        P("blk", "rep"),
        P(("blk", "rep"), None),
    )
    out_specs = (P("blk", None), P(("blk", "rep"), None))
    return jax.shard_map(local, mesh=mesh, in_specs=in_specs, out_specs=out_specs, check_vma=False)
```

```python
import functools
import math

import jax
import jax.numpy as jnp
from jax import lax
from jax.experimental import pallas as pl
from jax.experimental.pallas import tpu as pltpu
from jax.sharding import PartitionSpec as P

ITERS = 2
ROW_TILES = 16
F32 = jnp.float32
BF16 = jnp.bfloat16
VMEM_BYTES = 48 * 1024 * 1024
NT = (((1,), (1,)), ((), ()))
NN = (((1,), (0,)), ((), ()))


def dot(a, b, dims):
    return lax.dot_general(a, b, dims, preferred_element_type=F32)


def exact_dot(a, b):
    return lax.dot_general(a, b, NN, precision=lax.Precision.HIGHEST, preferred_element_type=F32)


def two_parts(value):
    high = value.astype(BF16)
    return high, (value - high.astype(F32)).astype(BF16)


def eliminate(work, spread):
    size = work.shape[0]
    for k in range(size // 8):
        at = size + 8 * k
        panel = work[8 * k : 8 * k + 8, :]
        shape = panel.shape
        for s in range(8):
            spread[k % 2, s] = jnp.broadcast_to(panel[:, at + s : at + s + 1], shape)
        d = {(i, s): jnp.broadcast_to(spread[k % 2, s, i : i + 1, :], shape) for s in range(8) for i in range(s, 8)}
        rows = [jnp.broadcast_to(work[8 * k + s : 8 * k + s + 1, :], shape) for s in range(8)]
        inverse = [None] * 8
        lower = {}
        for s in range(8):
            inverse[s] = 1.0 / d[s, s]
            for i in range(s + 1, 8):
                lower[i, s] = d[i, s] * inverse[s]
            for i in range(s + 1, 8):
                for j in range(s + 1, i + 1):
                    d[i, j] = d[i, j] - lower[i, s] * d[j, s]
                rows[i] = rows[i] - lower[i, s] * rows[s]
        for s in range(8):
            work[8 * k + s : 8 * k + s + 1, :] = (rows[s] * lax.rsqrt(d[s, s]))[0:1, :]
        solved = [rows[s] * inverse[s] for s in range(8)]
        below = [work[at : at + 8, :] for at in range(8 * k + 8, size, 8)]
        updated = list(below)
        for s in reversed(range(8)):
            for i in range(s):
                solved[i] = solved[i] - lower[s, i] * solved[s]
            for i, old in enumerate(below):
                updated[i] = updated[i] - jnp.broadcast_to(old[:, at + s : at + s + 1], shape) * solved[s]
        for i, new in enumerate(updated):
            work[8 * (k + 1 + i) : 8 * (k + 2 + i), :] = new
        yield


def run(steps):
    for _ in steps:
        pass


def put_identity(work):
    size = work.shape[0]
    row = lax.broadcasted_iota(jnp.int32, work.shape, 0)
    column = lax.broadcasted_iota(jnp.int32, work.shape, 1)
    work[...] = jnp.where(row == column, 1.0, 0.0).astype(F32)


def gather_gram(work, own_ref, other_ref, core):
    size = work.shape[0]
    half = size // 2
    put_identity(work)
    for source, at_core in ((own_ref, core), (other_ref, 1 - core)):
        total = jnp.zeros((half, 2 * size), F32)
        for b in range(source.shape[0]):
            total = total + source[b, 2 * size :, :].astype(F32)
        total = total + pltpu.roll(total, size, 1)
        at = pl.multiple_of(at_core * half, half)
        work[pl.ds(at, half), size:] = total[:, size:]


def gram_of_parts(parts):
    width = parts.shape[0] // 2
    full = dot(parts, parts, NT)
    full = full[0:width] + full[width:]
    return full + pltpu.roll(full, width, 1)


def apply_scale(scale_parts, value):
    high, low = two_parts(value)
    scale_high, scale_low = scale_parts
    return dot(
        jnp.concatenate([scale_high, scale_high, scale_low], axis=1),
        jnp.concatenate([high, low, high], axis=0),
        NN,
    )


def each(count, body, step=8):
    if count <= step:
        for i in range(count):
            body(i)
    else:

        def several(o, carry):
            for i in range(step):
                body(o * step + i)
            return carry

        lax.fori_loop(0, count // step, several, 0)


def beside(steps, tasks, count):
    if count > 8:
        run(steps)
        for task in tasks:
            each(count, task)
        return
    panels = 8
    done = 0
    for n in range(1, panels + 1):
        next(steps, None)
        while done < len(tasks) * count * n // panels:
            tasks[done // count](done % count)
            done += 1
    run(steps)


def pack_kernel(rows_hbm, cols_hbm, tiles_hbm, start_hbm, out_ref, start_out, rows_ref, cols_ref, tiles_ref, start_ref, sems):
    pairs = ((rows_hbm, rows_ref), (cols_hbm, cols_ref), (start_hbm, start_ref), (tiles_hbm, tiles_ref))
    copies = [pltpu.make_async_copy(source, to, sems.at[n]) for n, (source, to) in enumerate(pairs)]
    for copy in copies:
        copy.start()
    count, quarter, tile = tiles_ref.shape
    held = rows_ref.shape[1]
    lane = lax.broadcasted_iota(jnp.int32, (8, tile), 1)
    places = jnp.zeros((8, tile), jnp.int32)
    copies[0].wait()
    copies[1].wait()
    for j in range(held):
        places = jnp.where(lane == j, rows_ref[0, j], jnp.where(lane == held + j, cols_ref[0, j], places))
    places = places.astype(F32).astype(BF16)
    copies[2].wait()
    start_out[...] = start_ref[...].astype(BF16)
    copies[3].wait()

    def pack(i):
        out_ref[i] = jnp.concatenate([tiles_ref[i], places], axis=0)

    each(count, pack, 32)


def choose_kernel(place_ref, moved_ref, own_ref, near_ref, out_ref, places_ref):
    rep, block = place_ref[0], place_ref[1]
    core = lax.rem(rep, 2)
    blocks, _, tile = out_ref.shape
    width, share = own_ref.shape[1:]
    per_share = share // tile
    lane = lax.broadcasted_iota(jnp.int32, (8, tile), 1)

    def choose(b):
        for r in range(4):
            entry = moved_ref[b * 4 + r]
            entry = entry[entry.shape[0] - 8 :, :].astype(F32)
            places_ref[b * 4 + r] = entry.astype(jnp.int32)
        for x in range(2):
            entry = moved_ref[b * 4 + x * 2 + core]
            entry = entry[entry.shape[0] - 8 :, :].astype(F32)
            col = jnp.max(jnp.where(lane == blocks + block, entry, 0.0)).astype(jnp.int32)
            at = pl.multiple_of(lax.rem(col, per_share) * tile, tile)
            away = lax.bitwise_xor(lax.div(col, per_share), rep)
            far = lax.div(away, 2)
            mine = own_ref[far, :, pl.ds(at, tile)]
            theirs = near_ref[far, :, pl.ds(at, tile)]
            out_ref[b, x * width : (x + 1) * width, :] = jnp.where(lax.rem(away, 2) == 0, mine, theirs)

    each(blocks, choose)


def find_slots(cols_ref, slots_ref, first_at):
    blocks, group = cols_ref.shape

    def note(o):
        b = blocks - 1 - o
        for r in reversed(range(group)):
            first_at[cols_ref[b, r]] = b * group + r

    def look(b):
        for r in range(group):
            slots_ref[b, r] = first_at[cols_ref[b, r]]

    each(blocks, note)
    each(blocks, look)


def left_kernel(first, last, rows_ref, place_ref, tiles_own, tiles_near, own_ref, other_ref, out_ref, *rest):
    if last:
        raw_ref, *rest = rest
    total, stacked, packed, work, spread = rest
    core = lax.rem(place_ref[0], 2)
    pieces, _, tile = own_ref.shape
    width = total.shape[0]
    half = width // 2
    if not first:
        gather_gram(work, own_ref, other_ref, core)
    steps = eliminate(work, spread) if not first else iter(())
    total[...] = jnp.zeros_like(total)

    tasks = []
    for far in range(2):
        for source, stored, near in ((own_ref, tiles_own, 0), (other_ref, tiles_near, 1)):
            rep = lax.bitwise_xor(place_ref[0], 2 * far + near)

            def add(p, source=source, stored=stored, far=far, rep=rep):
                chosen = source[p, pl.ds(pl.multiple_of(lax.div(rep, 2) * width, width), width), :]
                product = dot(chosen, stored[far, p], NT)
                at = pl.multiple_of(rows_ref[rep, p] * tile, tile)
                total[:, pl.ds(at, tile)] += product

            tasks.append(add)
    beside(steps, tasks, pieces)
    value = total[...]
    if not first:
        value = apply_scale(two_parts(work[:, 0:width]), value)
    if last:
        raw_ref[...] = value
    high, low = two_parts(value)
    stacked[0:width, :] = high
    stacked[width:, :] = low
    pack_gram(gram_of_parts(stacked[...]), packed)
    mine = packed[pl.ds(pl.multiple_of(core * half, half), half), :]

    def send(p):
        for x in range(2):
            at = pl.multiple_of(rows_ref[x * 2 + core, p] * tile, tile)
            out_ref[p, x * width : (x + 1) * width, :] = stacked[0:width, pl.ds(at, tile)]
        out_ref[p, 2 * width :, :] = mine

    each(pieces, send)


def pack_gram(gram_twice, packed):
    high, low = two_parts(gram_twice)
    lane = lax.broadcasted_iota(jnp.int32, gram_twice.shape, 1)
    packed[...] = jnp.where(lane < gram_twice.shape[0], high.astype(F32), low.astype(F32)).astype(BF16)


def right_kernel(last, cols_ref, place_ref, tiles_own, tiles_near, own_ref, other_ref, out_ref, *rest):
    if last:
        total, scale_ref, *rest = rest
    else:
        total, *rest = rest
    stacked, packed, work, spread, quarters, slots_ref, first_at = rest
    find_slots(cols_ref, slots_ref, first_at)
    core = lax.rem(place_ref[0], 2)
    blocks, _, tile = own_ref.shape
    width = total.shape[0]
    half = width // 2
    quarter = quarters.shape[2]
    for far in range(2):
        for near, source in enumerate((tiles_own, tiles_near)):
            quarters[lax.bitwise_xor(place_ref[0], 2 * far + near)] = source[far, :, 0:quarter, :]

    def stored(b, r):
        return jnp.concatenate([quarters[q, b * 4 + r] for q in range(4)], axis=0)

    gather_gram(work, own_ref, other_ref, core)
    steps = eliminate(work, spread)
    total[...] = jnp.zeros_like(total)

    tasks = []
    for x in range(2):
        for source, at_core in ((own_ref, core), (other_ref, 1 - core)):

            def add(b, source=source, x=x, rep=x * 2 + at_core):
                product = dot(source[b, x * width : (x + 1) * width, :], stored(b, rep), NN)
                at = pl.multiple_of(slots_ref[b, rep] * tile, tile)
                total[:, pl.ds(at, tile)] += product

            tasks.append(add)
    beside(steps, tasks, blocks)
    scale = work[:, 0:width]
    scale_parts = two_parts(scale)
    chunk = 8 * tile

    def apply(o):
        at = o * chunk if isinstance(o, int) else pl.multiple_of(o * chunk, chunk)
        high, low = two_parts(apply_scale(scale_parts, total[:, pl.ds(at, chunk)]))
        stacked[0:width, pl.ds(at, chunk)] = high
        stacked[width:, pl.ds(at, chunk)] = low

    each(total.shape[1] // chunk, apply)
    gram = gram_of_parts(stacked[...])
    if last:
        scale_ref[...] = scale
        both = jnp.concatenate([gram[0:half, 0:width], gram[half:, 0:width]], axis=1)

        def send(b):
            out_ref[b] = both

        each(blocks, send)
        return
    pack_gram(gram, packed)
    mine = packed[pl.ds(pl.multiple_of(core * half, half), half), :]

    def send(b):
        for x in range(2):
            at = pl.multiple_of(slots_ref[b, x * 2 + core] * tile, tile)
            out_ref[b, x * width : (x + 1) * width, :] = stacked[0:width, pl.ds(at, tile)]
        out_ref[b, 2 * width :, :] = mine

    each(blocks, send)


def three_parts(value):
    high, low = two_parts(value)
    rest = value - high.astype(F32)
    return high, low, (rest - low.astype(F32)).astype(BF16)


def between_kernel(
    factor, cols_ref, place_ref, scale_ref, left_ref, total_ref, left_out, parts_ref, share, slots_ref, first_at
):
    width, tile = share.shape[0], total_ref.shape[1] // (slots_ref.shape[0] * 4)
    shares = share.shape[1] // tile
    find_slots(cols_ref, slots_ref, first_at)
    share[...] = jnp.zeros_like(share)

    def keep(b):
        for rep in range(4):
            col = cols_ref[b, rep]

            @pl.when(lax.div(col, shares) == place_ref[0])
            def _():
                to = pl.multiple_of(lax.rem(col, shares) * tile, tile)
                at = pl.multiple_of(slots_ref[b, rep] * tile, tile)
                share[:, pl.ds(to, tile)] = total_ref[:, pl.ds(at, tile)]

    each(slots_ref.shape[0], keep)
    high, middle, low = three_parts(share[...])
    for n, part in enumerate((high, middle, high, low, high, middle)):
        parts_ref[n * width : (n + 1) * width, :] = part
    left_out[...] = exact_dot(scale_ref[...] * factor, left_ref[...])


def finish_kernel(factor, gram_ref, scale_ref, parts_ref, right_hbm, work, spread, right, sems):
    width = scale_ref.shape[0]
    half = width // 2
    total = gram_ref[0]
    for b in range(1, gram_ref.shape[0]):
        total = total + gram_ref[b]
    put_identity(work)
    work[0:half, width:] = total[:, 0:width]
    work[half:, width:] = total[:, width:]
    run(eliminate(work, spread))
    high, middle, low = three_parts(exact_dot(work[:, 0:width], scale_ref[...]) * factor)
    scale = jnp.concatenate([high, high, middle, high, low, middle], axis=1)
    chunk = right.shape[1] // 4
    copies = []
    for n in range(4):
        at = pl.ds(n * chunk, chunk)
        right[:, at] = dot(scale, parts_ref[:, at], NN)
        copies.append(pltpu.make_async_copy(right.at[:, at], right_hbm.at[:, at], sems.at[n]))
        copies[-1].start()
    for copy in copies:
        copy.wait()


SMEM = pl.BlockSpec(memory_space=pltpu.SMEM)
VMEM = pl.BlockSpec(memory_space=pltpu.VMEM)
HBM = pl.BlockSpec(memory_space=pltpu.HBM)


def call(kernel, outs, smem, held, vmem, scratch=(), out_specs=None):
    return pl.pallas_call(
        kernel,
        out_shape=outs,
        in_specs=[SMEM] * len(smem) + [HBM] * len(held) + [VMEM] * len(vmem),
        out_specs=out_specs or [VMEM] * len(outs),
        scratch_shapes=list(scratch),
        compiler_params=pltpu.CompilerParams(vmem_limit_bytes=VMEM_BYTES),
    )(*smem, *[pltpu.with_memory_space_constraint(value, pltpu.HBM) for value in held], *vmem)


def local(tiles, tile_rows, tile_cols, start_right):
    blocks = lax.axis_size("blk")
    group = lax.axis_size("rep")
    block = lax.axis_index("blk")
    rep = lax.axis_index("rep").astype(jnp.int32)
    tile = tiles.shape[-1]
    share, width = start_right.shape
    flat_tiles = tiles.reshape(-1, tile, tile)
    held = flat_tiles.shape[0]
    quarter = tile // group
    total_rows = ROW_TILES * tile * blocks
    total_cols = share * group * blocks
    count = blocks * group
    place = jnp.stack([rep, block.astype(jnp.int32)])
    packed_rows = 2 * width + width // 2
    shape = jax.ShapeDtypeStruct

    def across(value):
        return lax.all_to_all(value, "blk", split_axis=0, concat_axis=0, tiled=True)

    def swap_x(value):
        return lax.ppermute(value, "rep", [(i, i ^ 2) for i in range(group)])

    def swap_core(value):
        return lax.ppermute(value, "rep", [(i, i ^ 1) for i in range(group)])

    moved, start = call(
        pack_kernel,
        [shape((count, quarter + 8, tile), BF16), shape((width, share), BF16)],
        [],
        [tile_rows, tile_cols, flat_tiles.reshape(count, quarter, tile), start_right.T],
        [],
        [
            pltpu.SMEM(tile_rows.shape, jnp.int32),
            pltpu.SMEM(tile_cols.shape, jnp.int32),
            pltpu.VMEM((count, quarter, tile), BF16),
            pltpu.VMEM((width, share), F32),
            pltpu.SemaphoreType.DMA((4,)),
        ],
    )
    start_own = jnp.stack([start, swap_x(start)])
    start_near = swap_core(start_own)
    tiles_own = jnp.stack([flat_tiles, swap_x(flat_tiles)])
    tiles_near = swap_core(tiles_own)
    moved = lax.all_to_all(moved, ("blk", "rep"), split_axis=0, concat_axis=0, tiled=True)
    chosen, places = call(
        choose_kernel,
        [shape((blocks, 2 * width, tile), BF16), shape((count, 8, tile), jnp.int32)],
        [place],
        [],
        [moved, start_own, start_near],
    )
    columns_own = jnp.stack([moved, swap_x(moved)])
    columns_near = swap_core(columns_own)
    places = places[:, 0, 0 : 2 * held].reshape(blocks, group, 2 * held)
    rows_all = lax.dynamic_index_in_dim(places, block, 0, keepdims=False)[:, 0:held]
    cols_here = lax.dynamic_index_in_dim(places, held + block, 2, keepdims=False)

    packed = pltpu.VMEM((width, 2 * width), BF16)
    work = pltpu.VMEM((width, 2 * width), F32)
    spread = pltpu.VMEM((2, 8, 8, 2 * width), F32)
    slot_scratch = [pltpu.SMEM((blocks, group), jnp.int32), pltpu.SMEM((share * group // tile,), jnp.int32)]
    for iteration in range(ITERS):
        first, last = iteration == 0, iteration == ITERS - 1
        chosen = across(chosen)
        outs = [shape((blocks, packed_rows, tile), BF16)]
        if last:
            outs.append(shape((width, ROW_TILES * tile), F32))
        results = call(
            functools.partial(left_kernel, first, last),
            outs,
            [rows_all, place],
            [],
            [tiles_own, tiles_near, chosen, swap_core(chosen)],
            [
                pltpu.VMEM((width, ROW_TILES * tile), F32),
                pltpu.VMEM((2 * width, ROW_TILES * tile), BF16),
                packed,
                work,
                spread,
            ],
        )
        picked = across(results[0])
        left_raw = results[-1]
        outs = [shape((blocks, packed_rows, tile), BF16)]
        if last:
            outs = [
                shape((blocks, width // 2, 2 * width), F32),
                shape((width, count * tile), F32),
                shape((width, width), F32),
            ]
        results = call(
            functools.partial(right_kernel, last),
            outs,
            [cols_here, place],
            [],
            [columns_own, columns_near, picked, swap_core(picked)],
            ([] if last else [pltpu.VMEM((width, count * tile), F32)])
            + [
                pltpu.VMEM((2 * width, count * tile), BF16),
                packed,
                work,
                spread,
            ]
            + [pltpu.VMEM((group, count, quarter, tile), BF16)]
            + slot_scratch,
        )
        chosen = results[0]
    gram, right_total, left_scale = results
    left, parts = call(
        functools.partial(between_kernel, math.sqrt(total_rows)),
        [shape(left_raw.shape, F32), shape((6 * width, share), BF16)],
        [cols_here, place],
        [],
        [left_scale, left_raw, right_total],
        [pltpu.VMEM((width, share), F32)] + slot_scratch,
    )
    (right,) = call(
        functools.partial(finish_kernel, math.sqrt(total_cols)),
        [shape((width, share), F32)],
        [],
        [],
        [across(gram), left_scale, parts],
        [work, spread, pltpu.VMEM((width, share), F32), pltpu.SemaphoreType.DMA((4,))],
        [HBM],
    )
    return (left.T, right.T)


def solution(mesh):
    in_specs = (
        P("blk", "rep", None, None),
        P("blk", "rep"),
        P("blk", "rep"),
        P(("blk", "rep"), None),
    )
    out_specs = (P("blk", None), P(("blk", "rep"), None))
    return jax.shard_map(local, mesh=mesh, in_specs=in_specs, out_specs=out_specs, check_vma=False)
```

```python
import functools
import math

import jax
import jax.numpy as jnp
from jax import lax
from jax.experimental import pallas as pl
from jax.experimental.pallas import tpu as pltpu
from jax.sharding import PartitionSpec as P

ITERS = 2
ROW_TILES = 16
F32 = jnp.float32
BF16 = jnp.bfloat16
MIB = 1024 * 1024
NT = (((1,), (1,)), ((), ()))
NN = (((1,), (0,)), ((), ()))


def dot(a, b, dims):
    return lax.dot_general(a, b, dims, preferred_element_type=F32)


def exact_dot(a, b):
    return lax.dot_general(a, b, NN, precision=lax.Precision.HIGHEST, preferred_element_type=F32)


def two_parts(value):
    high = value.astype(BF16)
    return high, (value - high.astype(F32)).astype(BF16)


def eliminate(work, spread):
    size = work.shape[0]
    for k in range(size // 8):
        at = size + 8 * k
        panel = work[8 * k : 8 * k + 8, :]
        shape = panel.shape
        for s in range(8):
            spread[k % 2, s] = jnp.broadcast_to(panel[:, at + s : at + s + 1], shape)
        d = {(i, s): jnp.broadcast_to(spread[k % 2, s, i : i + 1, :], shape) for s in range(8) for i in range(s, 8)}
        rows = [jnp.broadcast_to(work[8 * k + s : 8 * k + s + 1, :], shape) for s in range(8)]
        inverse = [None] * 8
        lower = {}
        for s in range(8):
            inverse[s] = 1.0 / d[s, s]
            for i in range(s + 1, 8):
                lower[i, s] = d[i, s] * inverse[s]
            for i in range(s + 1, 8):
                for j in range(s + 1, i + 1):
                    d[i, j] = d[i, j] - lower[i, s] * d[j, s]
                rows[i] = rows[i] - lower[i, s] * rows[s]
        for s in range(8):
            work[8 * k + s : 8 * k + s + 1, :] = (rows[s] * lax.rsqrt(d[s, s]))[0:1, :]
        solved = [rows[s] * inverse[s] for s in range(8)]
        below = [work[at : at + 8, :] for at in range(8 * k + 8, size, 8)]
        updated = list(below)
        for s in reversed(range(8)):
            for i in range(s):
                solved[i] = solved[i] - lower[s, i] * solved[s]
            for i, old in enumerate(below):
                updated[i] = updated[i] - jnp.broadcast_to(old[:, at + s : at + s + 1], shape) * solved[s]
        for i, new in enumerate(updated):
            work[8 * (k + 1 + i) : 8 * (k + 2 + i), :] = new
        yield


def run(steps):
    for _ in steps:
        pass


def put_identity(work):
    size = work.shape[0]
    row = lax.broadcasted_iota(jnp.int32, work.shape, 0)
    column = lax.broadcasted_iota(jnp.int32, work.shape, 1)
    work[...] = jnp.where(row == column, 1.0, 0.0).astype(F32)


def gather_gram(work, own_ref, other_ref, core):
    size = work.shape[0]
    half = size // 2
    put_identity(work)
    for source, at_core in ((own_ref, core), (other_ref, 1 - core)):
        total = jnp.zeros((half, 2 * size), F32)
        for b in range(source.shape[0]):
            total = total + source[b, 2 * size :, :].astype(F32)
        total = total + pltpu.roll(total, size, 1)
        at = pl.multiple_of(at_core * half, half)
        work[pl.ds(at, half), size:] = total[:, size:]


def gram_of_parts(parts):
    width = parts.shape[0] // 2
    full = dot(parts, parts, NT)
    full = full[0:width] + full[width:]
    return full + pltpu.roll(full, width, 1)


def apply_scale(scale_parts, value):
    high, low = two_parts(value)
    scale_high, scale_low = scale_parts
    return dot(
        jnp.concatenate([scale_high, scale_high, scale_low], axis=1),
        jnp.concatenate([high, low, high], axis=0),
        NN,
    )


def each(count, body, step=8):
    if count <= step:
        for i in range(count):
            body(i)
    else:

        def several(o, carry):
            for i in range(step):
                body(o * step + i)
            return carry

        lax.fori_loop(0, count // step, several, 0)


def beside(steps, tasks):
    if max(count for _, count in tasks) > 8:
        run(steps)
        for body, count in tasks:
            each(count, body)
        return
    tasks = [functools.partial(body, i) for body, count in tasks for i in range(count)]
    panels = 8
    for n in range(panels):
        next(steps, None)
        for task in tasks[len(tasks) * n // panels : len(tasks) * (n + 1) // panels]:
            task()
    run(steps)


def lanes(index, size):
    return pl.ds(index * size if isinstance(index, int) else pl.multiple_of(index * size, size), size)


def add_gram(total, raw_gram, chunk):
    def add(o):
        raw_gram[...] += gram_of_parts(jnp.concatenate(two_parts(total[:, lanes(o, chunk)]), axis=0))

    return add


def scaled_gram(scale, raw_gram):
    width = scale.shape[0]
    once = exact_dot(scale, raw_gram[:, 0:width])
    return lax.dot_general(
        once,
        jnp.concatenate([scale, scale], axis=0),
        NT,
        precision=lax.Precision.HIGHEST,
        preferred_element_type=F32,
    )


def pack_kernel(
    rows_hbm, cols_hbm, tiles_hbm, start_hbm, out_hbm, start_out, rows_ref, cols_ref, tiles_ref, start_ref, out_ref, sems
):
    pairs = ((rows_hbm, rows_ref), (cols_hbm, cols_ref), (tiles_hbm, tiles_ref), (start_hbm, start_ref))
    copies = [pltpu.make_async_copy(source, to, sems.at[n]) for n, (source, to) in enumerate(pairs)]
    for copy in copies:
        copy.start()
    count, quarter, tile = tiles_ref.shape
    held = rows_ref.shape[1]
    lane = lax.broadcasted_iota(jnp.int32, (8, tile), 1)
    places = jnp.zeros((8, tile), jnp.int32)
    copies[0].wait()
    copies[1].wait()
    for j in range(held):
        places = jnp.where(lane == j, rows_ref[0, j], jnp.where(lane == held + j, cols_ref[0, j], places))
    places = places.astype(F32).astype(BF16)
    copies[2].wait()

    def pack(i):
        out_ref[i] = jnp.concatenate([tiles_ref[i], places], axis=0)

    each(count, pack, 32)
    packed = pltpu.make_async_copy(out_ref, out_hbm, sems.at[4])
    packed.start()
    copies[3].wait()
    start_out[...] = start_ref[...].astype(BF16)
    packed.wait()


def choose_kernel(place_ref, moved_ref, own_ref, near_ref, out_hbm, places_ref, out_ref, sems):
    rep, block = place_ref[0], place_ref[1]
    core = lax.rem(rep, 2)
    blocks, _, tile = out_ref.shape
    width, share = own_ref.shape[1:]
    per_share = share // tile
    lane = lax.broadcasted_iota(jnp.int32, (8, tile), 1)

    def choose(b):
        for r in range(4):
            entry = moved_ref[b * 4 + r]
            entry = entry[entry.shape[0] - 8 :, :].astype(F32)
            places_ref[b * 4 + r] = entry.astype(jnp.int32)
        for x in range(2):
            entry = moved_ref[b * 4 + x * 2 + core]
            entry = entry[entry.shape[0] - 8 :, :].astype(F32)
            col = jnp.max(jnp.where(lane == blocks + block, entry, 0.0)).astype(jnp.int32)
            at = pl.multiple_of(lax.rem(col, per_share) * tile, tile)
            away = lax.bitwise_xor(lax.div(col, per_share), rep)
            far = lax.div(away, 2)
            mine = own_ref[far, :, pl.ds(at, tile)]
            theirs = near_ref[far, :, pl.ds(at, tile)]
            out_ref[b, x * width : (x + 1) * width, :] = jnp.where(lax.rem(away, 2) == 0, mine, theirs)
        pltpu.make_async_copy(out_ref.at[b], out_hbm.at[b], sems.at[b]).start()

    each(blocks, choose)
    for b in range(blocks):
        pltpu.make_async_copy(out_ref.at[b], out_hbm.at[b], sems.at[b]).wait()


def find_slots(cols_ref, slots_ref, first_at):
    blocks, group = cols_ref.shape

    def note(o):
        b = blocks - 1 - o
        for r in reversed(range(group)):
            first_at[cols_ref[b, r]] = b * group + r

    def look(b):
        for r in range(group):
            slots_ref[b, r] = first_at[cols_ref[b, r]]

    each(blocks, note)
    each(blocks, look)


def left_kernel(first, last, rows_ref, place_ref, tiles_own, tiles_near, own_ref, other_ref, out_ref, *rest):
    if last:
        raw_ref, *rest = rest
    total, stacked, packed, work, spread, raw_gram, *sems = rest
    core = lax.rem(place_ref[0], 2)
    pieces, _, tile = own_ref.shape
    width = total.shape[0]
    half = width // 2
    if not first:
        gather_gram(work, own_ref, other_ref, core)
    steps = eliminate(work, spread) if not first else iter(())
    total[...] = jnp.zeros_like(total)

    tasks = []
    for far in range(2):
        for source, stored, near in ((own_ref, tiles_own, 0), (other_ref, tiles_near, 1)):
            rep = lax.bitwise_xor(place_ref[0], 2 * far + near)

            def add(p, source=source, stored=stored, far=far, rep=rep):
                chosen = source[p, pl.ds(pl.multiple_of(lax.div(rep, 2) * width, width), width), :]
                product = dot(chosen, stored[far, p], NT)
                at = pl.multiple_of(rows_ref[rep, p] * tile, tile)
                total[:, pl.ds(at, tile)] += product

            tasks.append((add, pieces))
    chunk = 4 * tile
    if not first:
        raw_gram[...] = jnp.zeros_like(raw_gram)
        tasks.append((add_gram(total, raw_gram, chunk), total.shape[1] // chunk))
    beside(steps, tasks)
    mine = pl.ds(pl.multiple_of(core * half, half), half)
    if first:
        stacked[...] = jnp.concatenate(two_parts(total[...]), axis=0)
        copies = []
        for p in range(pieces):
            for x in range(2):
                at = pl.multiple_of(rows_ref[x * 2 + core, p] * tile, tile)
                copies.append(
                    pltpu.make_async_copy(
                        stacked.at[pl.ds(0, width), pl.ds(at, tile)],
                        out_ref.at[p, pl.ds(x * width, width), :],
                        sems[0].at[p, x],
                    )
                )
                copies[-1].start()
        pack_gram(gram_of_parts(stacked[...]), packed)
        for p in range(pieces):
            copies.append(
                pltpu.make_async_copy(packed.at[mine, :], out_ref.at[p, pl.ds(2 * width, half), :], sems[0].at[p, 2])
            )
            copies[-1].start()
        for copy in copies:
            copy.wait()
        return
    scale = work[:, 0:width]
    pack_gram(scaled_gram(scale, raw_gram), packed)
    scale = two_parts(scale)

    def apply(o):
        at = lanes(o, chunk)
        value = apply_scale(scale, total[:, at])
        if last:
            raw_ref[:, at] = value
        stacked[0:width, at] = value.astype(BF16)

    each(total.shape[1] // chunk, apply)
    mine = packed[mine, :]

    def send(p):
        for x in range(2):
            at = pl.multiple_of(rows_ref[x * 2 + core, p] * tile, tile)
            out_ref[p, x * width : (x + 1) * width, :] = stacked[0:width, pl.ds(at, tile)]
        out_ref[p, 2 * width :, :] = mine

    each(pieces, send)


def pack_gram(gram_twice, packed):
    high, low = two_parts(gram_twice)
    lane = lax.broadcasted_iota(jnp.int32, gram_twice.shape, 1)
    packed[...] = jnp.where(lane < gram_twice.shape[0], high.astype(F32), low.astype(F32)).astype(BF16)


def slots_kernel(cols_ref, slots_ref, first_at):
    find_slots(cols_ref, slots_ref, first_at)


def place_quarters(place_ref, tiles_own, tiles_near, quarters):
    quarter = quarters.shape[2]
    for far in range(2):
        for near, source in enumerate((tiles_own, tiles_near)):
            quarters[lax.bitwise_xor(place_ref[0], 2 * far + near)] = source[far, :, 0:quarter, :]


def right_tasks(place_ref, slots_ref, quarters, own_ref, other_ref, total, raw_gram):
    core = lax.rem(place_ref[0], 2)
    blocks, _, tile = own_ref.shape
    width = total.shape[0]
    total[...] = jnp.zeros_like(total)
    raw_gram[...] = jnp.zeros_like(raw_gram)
    tasks = []
    for x in range(2):
        for source, at_core in ((own_ref, core), (other_ref, 1 - core)):

            def add(b, source=source, x=x, rep=x * 2 + at_core):
                stored = jnp.concatenate([quarters[q, b * 4 + rep] for q in range(4)], axis=0)
                product = dot(source[b, x * width : (x + 1) * width, :], stored, NN)
                at = pl.multiple_of(slots_ref[b, rep] * tile, tile)
                total[:, pl.ds(at, tile)] += product

            tasks.append((add, blocks))
    chunk = 8 * tile
    tasks.append((add_gram(total, raw_gram, chunk), total.shape[1] // chunk))
    return tasks


def right_kernel(
    cols_ref,
    place_ref,
    tiles_own,
    tiles_near,
    own_ref,
    other_ref,
    out_ref,
    total,
    stacked,
    packed,
    work,
    spread,
    raw_gram,
    quarters,
    slots_ref,
    first_at,
):
    find_slots(cols_ref, slots_ref, first_at)
    core = lax.rem(place_ref[0], 2)
    blocks, _, tile = own_ref.shape
    width = total.shape[0]
    half = width // 2
    place_quarters(place_ref, tiles_own, tiles_near, quarters)
    gather_gram(work, own_ref, other_ref, core)
    beside(
        eliminate(work, spread), right_tasks(place_ref, slots_ref, quarters, own_ref, other_ref, total, raw_gram)
    )
    scale = work[:, 0:width]
    pack_gram(scaled_gram(scale, raw_gram), packed)
    scale_parts = two_parts(scale)
    chunk = 8 * tile

    def apply(o):
        at = lanes(o, chunk)
        stacked[0:width, at] = apply_scale(scale_parts, total[:, at]).astype(BF16)

    each(total.shape[1] // chunk, apply)
    mine = packed[pl.ds(pl.multiple_of(core * half, half), half), :]

    def send(b):
        for x in range(2):
            at = pl.multiple_of(slots_ref[b, x * 2 + core] * tile, tile)
            out_ref[b, x * width : (x + 1) * width, :] = stacked[0:width, pl.ds(at, tile)]
        out_ref[b, 2 * width :, :] = mine

    each(blocks, send)


def last_right_kernel(
    slots_ref, place_ref, tiles_own, tiles_near, own_ref, other_ref, gram_hbm, total, raw_gram, quarters, sems
):
    place_quarters(place_ref, tiles_own, tiles_near, quarters)
    beside(iter(()), right_tasks(place_ref, slots_ref, quarters, own_ref, other_ref, total, raw_gram))
    width = total.shape[0]
    half = width // 2
    lane = lax.broadcasted_iota(jnp.int32, (half, 2 * width), 1)
    raw_gram[0:half, :] = jnp.where(lane < width, raw_gram[0:half, :], raw_gram[half:, :])
    copies = [
        pltpu.make_async_copy(raw_gram.at[pl.ds(0, half), :], gram_hbm.at[b], sems.at[b])
        for b in range(gram_hbm.shape[0])
    ]
    for copy in copies:
        copy.start()
    for copy in copies:
        copy.wait()


def between_kernel(
    left_factor,
    right_factor,
    cols_ref,
    slots_ref,
    place_ref,
    tiles_own,
    tiles_near,
    own_ref,
    other_ref,
    left_ref,
    left_out,
    parts_ref,
    scale_ref,
    share,
    work,
    spread,
    total_ref,
    raw_gram,
    quarters,
):
    place_quarters(place_ref, tiles_own, tiles_near, quarters)
    gather_gram(work, own_ref, other_ref, lax.rem(place_ref[0], 2))
    products = right_tasks(place_ref, slots_ref, quarters, own_ref, other_ref, total_ref, raw_gram)[:-1]
    beside(eliminate(work, spread), products)
    scale_ref[...] = work[:, 0 : scale_ref.shape[1]]
    left_out[...] = exact_dot(scale_ref[...] * left_factor, left_ref[...])
    width, tile = share.shape[0], total_ref.shape[1] // (slots_ref.shape[0] * 4)
    shares = share.shape[1] // tile
    share[...] = jnp.zeros_like(share)

    def keep(b):
        for rep in range(4):
            col = cols_ref[b, rep]

            @pl.when(lax.div(col, shares) == place_ref[0])
            def _():
                to = pl.multiple_of(lax.rem(col, shares) * tile, tile)
                at = pl.multiple_of(slots_ref[b, rep] * tile, tile)
                share[:, pl.ds(to, tile)] = total_ref[:, pl.ds(at, tile)]

    each(slots_ref.shape[0], keep)
    for n, part in enumerate(two_parts(apply_scale(two_parts(scale_ref[...] * right_factor), share[...]))):
        parts_ref[n * width : (n + 1) * width, :] = part


def finish_kernel(gram_ref, scale_ref, parts_ref, right_hbm, work, spread, right, sems):
    width = scale_ref.shape[0]
    half = width // 2
    total = gram_ref[0]
    for b in range(1, gram_ref.shape[0]):
        total = total + gram_ref[b]
    gram = scaled_gram(scale_ref[...], jnp.concatenate([total[:, 0:width], total[:, width:]], axis=0))
    put_identity(work)
    work[:, width:] = gram[:, width:]
    run(eliminate(work, spread))
    high, low = two_parts(work[:, 0:width])
    scale = jnp.concatenate([high, high], axis=1)
    chunk = right.shape[1] // 4
    copies = []
    for n in range(4):
        at = pl.ds(n * chunk, chunk)
        right[:, at] = dot(scale, parts_ref[:, at], NN) + dot(low, parts_ref[0:width, at], NN)
        copies.append(pltpu.make_async_copy(right.at[:, at], right_hbm.at[:, at], sems.at[n]))
        copies[-1].start()
    for copy in copies:
        copy.wait()


SMEM = pl.BlockSpec(memory_space=pltpu.SMEM)
VMEM = pl.BlockSpec(memory_space=pltpu.VMEM)
HBM = pl.BlockSpec(memory_space=pltpu.HBM)


def call(kernel, outs, smem, held, vmem, scratch=(), out_specs=None):
    held = [pltpu.with_memory_space_constraint(value, pltpu.HBM) for value in held]
    return pl.pallas_call(
        kernel,
        out_shape=outs,
        in_specs=[SMEM] * len(smem) + [HBM] * len(held) + [VMEM] * len(vmem),
        out_specs=out_specs or [VMEM] * len(outs),
        scratch_shapes=list(scratch),
        compiler_params=pltpu.CompilerParams(vmem_limit_bytes=min(48, lax.axis_size("blk") + 8) * MIB),
    )(*smem, *held, *vmem)


def local(tiles, tile_rows, tile_cols, start_right):
    blocks = lax.axis_size("blk")
    group = lax.axis_size("rep")
    block = lax.axis_index("blk")
    rep = lax.axis_index("rep").astype(jnp.int32)
    tile = tiles.shape[-1]
    share, width = start_right.shape
    flat_tiles = tiles.reshape(-1, tile, tile)
    held = flat_tiles.shape[0]
    quarter = tile // group
    total_rows = ROW_TILES * tile * blocks
    total_cols = share * group * blocks
    count = blocks * group
    place = jnp.stack([rep, block.astype(jnp.int32)])
    packed_rows = 2 * width + width // 2
    shape = jax.ShapeDtypeStruct

    def across(value):
        return lax.all_to_all(value, "blk", split_axis=0, concat_axis=0, tiled=True)

    def swap_x(value):
        return lax.ppermute(value, "rep", [(i, i ^ 2) for i in range(group)])

    def swap_core(value):
        return lax.ppermute(value, "rep", [(i, i ^ 1) for i in range(group)])

    moved, start = call(
        pack_kernel,
        [shape((count, quarter + 8, tile), BF16), shape((width, share), BF16)],
        [],
        [tile_rows, tile_cols, flat_tiles.reshape(count, quarter, tile), start_right.T],
        [],
        [
            pltpu.SMEM(tile_rows.shape, jnp.int32),
            pltpu.SMEM(tile_cols.shape, jnp.int32),
            pltpu.VMEM((count, quarter, tile), BF16),
            pltpu.VMEM((width, share), F32),
            pltpu.VMEM((count, quarter + 8, tile), BF16),
            pltpu.SemaphoreType.DMA((5,)),
        ],
        [HBM, VMEM],
    )
    start_own = jnp.stack([start, swap_x(start)])
    start_near = swap_core(start_own)
    moved = lax.all_to_all(moved, ("blk", "rep"), split_axis=0, concat_axis=0, tiled=True)
    chosen, places = call(
        choose_kernel,
        [shape((blocks, 2 * width, tile), BF16), shape((count, 8, tile), jnp.int32)],
        [place],
        [],
        [moved, start_own, start_near],
        [pltpu.VMEM((blocks, 2 * width, tile), BF16), pltpu.SemaphoreType.DMA((blocks,))],
        [HBM, VMEM],
    )
    flat_tiles, moved = lax.optimization_barrier((flat_tiles, moved))
    tiles_own = jnp.stack([flat_tiles, swap_x(flat_tiles)])
    tiles_near = swap_core(tiles_own)
    columns_own = jnp.stack([moved, swap_x(moved)])
    columns_near = swap_core(columns_own)
    places = places[:, 0, 0 : 2 * held].reshape(blocks, group, 2 * held)
    rows_all = lax.dynamic_index_in_dim(places, block, 0, keepdims=False)[:, 0:held]
    cols_here = lax.dynamic_index_in_dim(places, held + block, 2, keepdims=False)

    packed = pltpu.VMEM((width, 2 * width), BF16)
    work = pltpu.VMEM((width, 2 * width), F32)
    spread = pltpu.VMEM((2, 8, 8, 2 * width), F32)
    slot_scratch = [pltpu.SMEM((blocks, group), jnp.int32), pltpu.SMEM((share * group // tile,), jnp.int32)]
    for iteration in range(ITERS):
        first, last = iteration == 0, iteration == ITERS - 1
        chosen = across(chosen)
        outs = [shape((blocks, packed_rows, tile), BF16)]
        if last:
            outs.append(shape((width, ROW_TILES * tile), F32))
        results = call(
            functools.partial(left_kernel, first, last),
            outs,
            [rows_all, place],
            [],
            [tiles_own, tiles_near, chosen, swap_core(chosen)],
            [
                pltpu.VMEM((width, ROW_TILES * tile), F32),
                pltpu.VMEM((2 * width if first else width, ROW_TILES * tile), BF16),
                packed,
                work,
                spread,
                pltpu.VMEM((width, 2 * width), F32),
            ]
            + ([pltpu.SemaphoreType.DMA((blocks, 3))] if first else []),
            [HBM] if first else None,
        )
        picked = across(results[0])
        left_raw = results[-1]
        total = pltpu.VMEM((width, count * tile), F32)
        gram_scratch = pltpu.VMEM((width, 2 * width), F32)
        quarters = pltpu.VMEM((group, count, quarter, tile), BF16)
        other = swap_core(picked)
        if last:
            break
        (chosen,) = call(
            right_kernel,
            [shape((blocks, packed_rows, tile), BF16)],
            [cols_here, place],
            [],
            [columns_own, columns_near, picked, other],
            [total, pltpu.VMEM((width, count * tile), BF16), packed, work, spread, gram_scratch, quarters]
            + slot_scratch,
        )
    (slots,) = call(
        slots_kernel,
        [shape(cols_here.shape, jnp.int32)],
        [cols_here],
        [],
        [],
        slot_scratch[1:],
        [SMEM],
    )
    (gram,) = call(
        last_right_kernel,
        [shape((blocks, width // 2, 2 * width), F32)],
        [slots, place],
        [],
        [columns_own, columns_near, picked, other],
        [total, gram_scratch, quarters, pltpu.SemaphoreType.DMA((blocks,))],
        [HBM],
    )
    left, parts, left_scale = call(
        functools.partial(between_kernel, math.sqrt(total_rows), math.sqrt(total_cols)),
        [shape(left_raw.shape, F32), shape((2 * width, share), BF16), shape((width, width), F32)],
        [cols_here, slots, place],
        [],
        [columns_own, columns_near, picked, other, left_raw],
        [pltpu.VMEM((width, share), F32), work, spread, total, gram_scratch, quarters],
    )
    (right,) = call(
        finish_kernel,
        [shape((width, share), F32)],
        [],
        [],
        [across(gram), left_scale, parts],
        [work, spread, pltpu.VMEM((width, share), F32), pltpu.SemaphoreType.DMA((4,))],
        [HBM],
    )
    return (left.T, right.T)


def solution(mesh):
    in_specs = (
        P("blk", "rep", None, None),
        P("blk", "rep"),
        P("blk", "rep"),
        P(("blk", "rep"), None),
    )
    out_specs = (P("blk", None), P(("blk", "rep"), None))
    return jax.shard_map(local, mesh=mesh, in_specs=in_specs, out_specs=out_specs, check_vma=False)
```

```python
import functools
import math

import jax
import jax.numpy as jnp
from jax import lax
from jax.experimental import pallas as pl
from jax.experimental.pallas import tpu as pltpu
from jax.sharding import PartitionSpec as P

ITERS = 2
ROW_TILES = 16
F32 = jnp.float32
BF16 = jnp.bfloat16
MIB = 1024 * 1024
NT = (((1,), (1,)), ((), ()))
NN = (((1,), (0,)), ((), ()))


def dot(a, b, dims):
    return lax.dot_general(a, b, dims, preferred_element_type=F32)


def exact_dot(a, b):
    return lax.dot_general(a, b, NN, precision=lax.Precision.HIGHEST, preferred_element_type=F32)


def two_parts(value):
    high = value.astype(BF16)
    return high, (value - high.astype(F32)).astype(BF16)


def eliminate(work, spread):
    size = work.shape[0]
    for k in range(size // 8):
        at = size + 8 * k
        panel = work[8 * k : 8 * k + 8, :]
        shape = panel.shape
        for s in range(8):
            spread[k % 2, s] = jnp.broadcast_to(panel[:, at + s : at + s + 1], shape)
        d = {(i, s): jnp.broadcast_to(spread[k % 2, s, i : i + 1, :], shape) for s in range(8) for i in range(s, 8)}
        rows = [jnp.broadcast_to(work[8 * k + s : 8 * k + s + 1, :], shape) for s in range(8)]
        inverse = [None] * 8
        lower = {}
        for s in range(8):
            inverse[s] = 1.0 / d[s, s]
            for i in range(s + 1, 8):
                lower[i, s] = d[i, s] * inverse[s]
            for i in range(s + 1, 8):
                for j in range(s + 1, i + 1):
                    d[i, j] = d[i, j] - lower[i, s] * d[j, s]
                rows[i] = rows[i] - lower[i, s] * rows[s]
        for s in range(8):
            work[8 * k + s : 8 * k + s + 1, :] = (rows[s] * lax.rsqrt(d[s, s]))[0:1, :]
        solved = [rows[s] * inverse[s] for s in range(8)]
        below = [work[at : at + 8, :] for at in range(8 * k + 8, size, 8)]
        updated = list(below)
        for s in reversed(range(8)):
            for i in range(s):
                solved[i] = solved[i] - lower[s, i] * solved[s]
            for i, old in enumerate(below):
                updated[i] = updated[i] - jnp.broadcast_to(old[:, at + s : at + s + 1], shape) * solved[s]
        for i, new in enumerate(updated):
            work[8 * (k + 1 + i) : 8 * (k + 2 + i), :] = new
        yield


def run(steps):
    for _ in steps:
        pass


def put_identity(work):
    size = work.shape[0]
    row = lax.broadcasted_iota(jnp.int32, work.shape, 0)
    column = lax.broadcasted_iota(jnp.int32, work.shape, 1)
    work[...] = jnp.where(row == column, 1.0, 0.0).astype(F32)


def gather_gram(work, own_ref, other_ref, core):
    size = work.shape[0]
    half = size // 2
    put_identity(work)
    for source, at_core in ((own_ref, core), (other_ref, 1 - core)):
        total = jnp.zeros((half, 2 * size), F32)
        for b in range(source.shape[0]):
            total = total + source[b, 2 * size :, :].astype(F32)
        total = total + pltpu.roll(total, size, 1)
        at = pl.multiple_of(at_core * half, half)
        work[pl.ds(at, half), size:] = total[:, size:]


def gram_of_parts(parts):
    width = parts.shape[0] // 2
    full = dot(parts, parts, NT)
    full = full[0:width] + full[width:]
    return full + pltpu.roll(full, width, 1)


def apply_scale(scale_parts, value):
    high, low = two_parts(value)
    scale_high, scale_low = scale_parts
    return dot(
        jnp.concatenate([scale_high, scale_high, scale_low], axis=1),
        jnp.concatenate([high, low, high], axis=0),
        NN,
    )


def each(count, body, step=8):
    if count <= step:
        for i in range(count):
            body(i)
    else:

        def several(o, carry):
            for i in range(step):
                body(o * step + i)
            return carry

        lax.fori_loop(0, count // step, several, 0)


def beside(steps, ready, tasks):
    next(steps, None)
    ready()
    if max(count for _, count in tasks) > 8:
        run(steps)
        for body, count in tasks:
            each(count, body)
        return
    tasks = [functools.partial(body, i) for body, count in tasks for i in range(count)]
    panels = 8
    for n in range(panels):
        for task in tasks[len(tasks) * n // panels : len(tasks) * (n + 1) // panels]:
            task()
        next(steps, None)
    run(steps)


def lanes(index, size):
    return pl.ds(index * size if isinstance(index, int) else pl.multiple_of(index * size, size), size)


def add_gram(total, raw_gram, chunk):
    def add(o):
        raw_gram[...] += gram_of_parts(jnp.concatenate(two_parts(total[:, lanes(o, chunk)]), axis=0))

    return add


def scaled_gram(scale, raw_gram):
    width = scale.shape[0]
    once = exact_dot(scale, raw_gram[:, 0:width])
    return lax.dot_general(
        once,
        jnp.concatenate([scale, scale], axis=0),
        NT,
        precision=lax.Precision.HIGHEST,
        preferred_element_type=F32,
    )


def pack_kernel(
    rows_hbm, cols_hbm, tiles_hbm, start_hbm, out_ref, start_out, rows_ref, cols_ref, tiles_ref, start_ref, sems
):
    pairs = ((rows_hbm, rows_ref), (cols_hbm, cols_ref), (tiles_hbm, tiles_ref), (start_hbm, start_ref))
    copies = [pltpu.make_async_copy(source, to, sems.at[n]) for n, (source, to) in enumerate(pairs)]
    for copy in copies:
        copy.start()
    count, quarter, tile = tiles_ref.shape
    held = rows_ref.shape[1]
    lane = lax.broadcasted_iota(jnp.int32, (8, tile), 1)
    places = jnp.zeros((8, tile), jnp.int32)
    copies[0].wait()
    copies[1].wait()
    for j in range(held):
        places = jnp.where(lane == j, rows_ref[0, j], jnp.where(lane == held + j, cols_ref[0, j], places))
    places = places.astype(F32).astype(BF16)
    copies[2].wait()

    def pack(i):
        out_ref[i] = jnp.concatenate([tiles_ref[i], places], axis=0)

    each(count, pack, 32)
    copies[3].wait()
    start_out[...] = start_ref[...].astype(BF16)


def choose_kernel(moved_ref, own_ref, near_ref, out_hbm, places_ref, out_ref, sems):
    rep, block = lax.axis_index("rep"), lax.axis_index("blk")
    core = lax.rem(rep, 2)
    blocks, _, tile = out_ref.shape
    width, share = own_ref.shape[1:]
    per_share = share // tile
    lane = lax.broadcasted_iota(jnp.int32, (8, tile), 1)

    def choose(b):
        for r in range(4):
            entry = moved_ref[b * 4 + r]
            entry = entry[entry.shape[0] - 8 :, :].astype(F32)
            places_ref[b * 4 + r] = entry.astype(jnp.int32)
        for x in range(2):
            entry = moved_ref[b * 4 + x * 2 + core]
            entry = entry[entry.shape[0] - 8 :, :].astype(F32)
            col = jnp.max(jnp.where(lane == blocks + block, entry, 0.0)).astype(jnp.int32)
            at = pl.multiple_of(lax.rem(col, per_share) * tile, tile)
            away = lax.bitwise_xor(lax.div(col, per_share), rep)
            far = lax.div(away, 2)
            mine = own_ref[far, :, pl.ds(at, tile)]
            theirs = near_ref[far, :, pl.ds(at, tile)]
            out_ref[b, x * width : (x + 1) * width, :] = jnp.where(lax.rem(away, 2) == 0, mine, theirs)
        pltpu.make_async_copy(out_ref.at[b], out_hbm.at[b], sems.at[b]).start()

    each(blocks, choose)
    for b in range(blocks):
        pltpu.make_async_copy(out_ref.at[b], out_hbm.at[b], sems.at[b]).wait()


def find_slots(cols_ref, slots_ref, first_at):
    blocks, group = cols_ref.shape

    def note(o):
        b = blocks - 1 - o
        for r in reversed(range(group)):
            first_at[cols_ref[b, r]] = b * group + r

    def look(b):
        for r in range(group):
            slots_ref[b, r] = first_at[cols_ref[b, r]]

    each(blocks, note)
    each(blocks, look)


def left_kernel(first, last, rows_vmem, tiles_own, tiles_near, own_ref, other_ref, out_ref, *rest):
    if last:
        raw_ref, *rest = rest
    total, stacked, packed, work, spread, raw_gram, rows_ref, rows_sem, *rest = rest
    rows = pltpu.make_async_copy(rows_vmem, rows_ref, rows_sem.at[0])
    rows.start()
    this = lax.axis_index("rep")
    core = lax.rem(this, 2)
    pieces, _, tile = own_ref.shape
    width = total.shape[0]
    half = width // 2
    if not first:
        gather_gram(work, own_ref, other_ref, core)
    steps = eliminate(work, spread) if not first else iter(())
    total[...] = jnp.zeros_like(total)

    early = first and pieces <= 8
    if first:
        sems, *rest = rest
    if early:
        (products,) = rest
    tasks = []
    for far in range(2):
        for source, stored, near in ((own_ref, tiles_own, 0), (other_ref, tiles_near, 1)):
            rep = lax.bitwise_xor(this, 2 * far + near)

            def multiply(p, source=source, stored=stored, far=far, rep=rep):
                chosen = source[p, pl.ds(pl.multiple_of(lax.div(rep, 2) * width, width), width), :]
                return dot(chosen, stored[far, p], NT)

            def add(p, rep=rep, multiply=multiply, kept=2 * far + near):
                product = products[kept, p] if early else multiply(p)
                at = pl.multiple_of(rows_ref[rep, p] * tile, tile)
                total[:, pl.ds(at, tile)] += product

            tasks.append((add, pieces))
            if early:
                for p in range(pieces):
                    products[2 * far + near, p] = multiply(p)
    chunk = 4 * tile
    if not first:
        raw_gram[...] = jnp.zeros_like(raw_gram)
        tasks.append((add_gram(total, raw_gram, chunk), total.shape[1] // chunk))
    beside(steps, rows.wait, tasks)
    mine = pl.ds(pl.multiple_of(core * half, half), half)
    if first:
        stacked[...] = jnp.concatenate(two_parts(total[...]), axis=0)
        copies = []
        for p in range(pieces):
            for x in range(2):
                at = pl.multiple_of(rows_ref[x * 2 + core, p] * tile, tile)
                copies.append(
                    pltpu.make_async_copy(
                        stacked.at[pl.ds(0, width), pl.ds(at, tile)],
                        out_ref.at[p, pl.ds(x * width, width), :],
                        sems.at[p, x],
                    )
                )
                copies[-1].start()
        pack_gram(gram_of_parts(stacked[...]), packed)
        for p in range(pieces):
            copies.append(
                pltpu.make_async_copy(packed.at[mine, :], out_ref.at[p, pl.ds(2 * width, half), :], sems.at[p, 2])
            )
            copies[-1].start()
        for copy in copies:
            copy.wait()
        return
    scale = work[:, 0:width]
    pack_gram(scaled_gram(scale, raw_gram), packed)
    scale = two_parts(scale)

    def apply(o):
        at = lanes(o, chunk)
        value = apply_scale(scale, total[:, at])
        if last:
            raw_ref[:, at] = value
        stacked[0:width, at] = value.astype(BF16)

    each(total.shape[1] // chunk, apply)
    mine = packed[mine, :]

    def send(p):
        for x in range(2):
            at = pl.multiple_of(rows_ref[x * 2 + core, p] * tile, tile)
            out_ref[p, x * width : (x + 1) * width, :] = stacked[0:width, pl.ds(at, tile)]
        out_ref[p, 2 * width :, :] = mine

    each(pieces, send)


def pack_gram(gram_twice, packed):
    high, low = two_parts(gram_twice)
    lane = lax.broadcasted_iota(jnp.int32, gram_twice.shape, 1)
    packed[...] = jnp.where(lane < gram_twice.shape[0], high.astype(F32), low.astype(F32)).astype(BF16)


def slots_kernel(cols_ref, slots_ref, first_at):
    find_slots(cols_ref, slots_ref, first_at)


def place_quarters(tiles_own, tiles_near, quarters):
    quarter = quarters.shape[2]
    for far in range(2):
        for near, source in enumerate((tiles_own, tiles_near)):
            quarters[lax.bitwise_xor(lax.axis_index("rep"), 2 * far + near)] = source[far, :, 0:quarter, :]


def right_tasks(slots_ref, quarters, own_ref, other_ref, total, raw_gram):
    core = lax.rem(lax.axis_index("rep"), 2)
    blocks, _, tile = own_ref.shape
    width = total.shape[0]
    total[...] = jnp.zeros_like(total)
    raw_gram[...] = jnp.zeros_like(raw_gram)
    tasks = []
    for x in range(2):
        for source, at_core in ((own_ref, core), (other_ref, 1 - core)):

            def add(b, source=source, x=x, rep=x * 2 + at_core):
                stored = jnp.concatenate([quarters[q, b * 4 + rep] for q in range(4)], axis=0)
                product = dot(source[b, x * width : (x + 1) * width, :], stored, NN)
                at = pl.multiple_of(slots_ref[b, rep] * tile, tile)
                total[:, pl.ds(at, tile)] += product

            tasks.append((add, blocks))
    chunk = 8 * tile
    tasks.append((add_gram(total, raw_gram, chunk), total.shape[1] // chunk))
    return tasks


def right_kernel(
    cols_vmem,
    tiles_own,
    tiles_near,
    own_ref,
    other_ref,
    out_ref,
    total,
    stacked,
    packed,
    work,
    spread,
    raw_gram,
    quarters,
    cols_ref,
    cols_sem,
    slots_ref,
    first_at,
):
    cols = pltpu.make_async_copy(cols_vmem, cols_ref, cols_sem.at[0])
    cols.start()
    core = lax.rem(lax.axis_index("rep"), 2)
    blocks, _, tile = own_ref.shape
    width = total.shape[0]
    half = width // 2
    place_quarters(tiles_own, tiles_near, quarters)
    gather_gram(work, own_ref, other_ref, core)

    def ready():
        cols.wait()
        find_slots(cols_ref, slots_ref, first_at)

    tasks = right_tasks(slots_ref, quarters, own_ref, other_ref, total, raw_gram)
    beside(eliminate(work, spread), ready, tasks)
    scale = work[:, 0:width]
    pack_gram(scaled_gram(scale, raw_gram), packed)
    scale_parts = two_parts(scale)
    chunk = 8 * tile

    def apply(o):
        at = lanes(o, chunk)
        stacked[0:width, at] = apply_scale(scale_parts, total[:, at]).astype(BF16)

    each(total.shape[1] // chunk, apply)
    mine = packed[pl.ds(pl.multiple_of(core * half, half), half), :]

    def send(b):
        for x in range(2):
            at = pl.multiple_of(slots_ref[b, x * 2 + core] * tile, tile)
            out_ref[b, x * width : (x + 1) * width, :] = stacked[0:width, pl.ds(at, tile)]
        out_ref[b, 2 * width :, :] = mine

    each(blocks, send)


def last_right_kernel(
    slots_vmem, tiles_own, tiles_near, own_ref, other_ref, gram_hbm, total, raw_gram, quarters, slots_ref, sems
):
    slots = pltpu.make_async_copy(slots_vmem, slots_ref, sems.at[gram_hbm.shape[0]])
    slots.start()
    place_quarters(tiles_own, tiles_near, quarters)
    tasks = right_tasks(slots_ref, quarters, own_ref, other_ref, total, raw_gram)
    beside(iter(()), slots.wait, tasks)
    width = total.shape[0]
    half = width // 2
    lane = lax.broadcasted_iota(jnp.int32, (half, 2 * width), 1)
    raw_gram[0:half, :] = jnp.where(lane < width, raw_gram[0:half, :], raw_gram[half:, :])
    copies = [
        pltpu.make_async_copy(raw_gram.at[pl.ds(0, half), :], gram_hbm.at[b], sems.at[b])
        for b in range(gram_hbm.shape[0])
    ]
    for copy in copies:
        copy.start()
    for copy in copies:
        copy.wait()


def between_kernel(
    left_factor,
    right_factor,
    cols_ref,
    slots_ref,
    tiles_own,
    tiles_near,
    own_ref,
    other_ref,
    left_ref,
    left_out,
    parts_ref,
    scale_ref,
    share,
    work,
    spread,
    total_ref,
    raw_gram,
    quarters,
):
    place_quarters(tiles_own, tiles_near, quarters)
    gather_gram(work, own_ref, other_ref, lax.rem(lax.axis_index("rep"), 2))
    products = right_tasks(slots_ref, quarters, own_ref, other_ref, total_ref, raw_gram)[:-1]
    beside(eliminate(work, spread), lambda: None, products)
    scale_ref[...] = work[:, 0 : scale_ref.shape[1]]
    left_out[...] = exact_dot(scale_ref[...] * left_factor, left_ref[...])
    width, tile = share.shape[0], total_ref.shape[1] // (slots_ref.shape[0] * 4)
    shares = share.shape[1] // tile
    share[...] = jnp.zeros_like(share)

    def keep(b):
        for rep in range(4):
            col = cols_ref[b, rep]

            @pl.when(lax.div(col, shares) == lax.axis_index("rep"))
            def _():
                to = pl.multiple_of(lax.rem(col, shares) * tile, tile)
                at = pl.multiple_of(slots_ref[b, rep] * tile, tile)
                share[:, pl.ds(to, tile)] = total_ref[:, pl.ds(at, tile)]

    each(slots_ref.shape[0], keep)
    for n, part in enumerate(two_parts(apply_scale(two_parts(scale_ref[...] * right_factor), share[...]))):
        parts_ref[n * width : (n + 1) * width, :] = part


def finish_kernel(gram_ref, scale_ref, parts_ref, right_hbm, work, spread, right, sems):
    width = scale_ref.shape[0]
    half = width // 2
    total = gram_ref[0]
    for b in range(1, gram_ref.shape[0]):
        total = total + gram_ref[b]
    gram = scaled_gram(scale_ref[...], jnp.concatenate([total[:, 0:width], total[:, width:]], axis=0))
    put_identity(work)
    work[:, width:] = gram[:, width:]
    run(eliminate(work, spread))
    high, low = two_parts(work[:, 0:width])
    scale = jnp.concatenate([high, high], axis=1)
    chunk = right.shape[1] // 4
    copies = []
    for n in range(4):
        at = pl.ds(n * chunk, chunk)
        right[:, at] = dot(scale, parts_ref[:, at], NN) + dot(low, parts_ref[0:width, at], NN)
        copies.append(pltpu.make_async_copy(right.at[:, at], right_hbm.at[:, at], sems.at[n]))
        copies[-1].start()
    for copy in copies:
        copy.wait()


SMEM = pl.BlockSpec(memory_space=pltpu.SMEM)
VMEM = pl.BlockSpec(memory_space=pltpu.VMEM)
HBM = pl.BlockSpec(memory_space=pltpu.HBM)


def call(kernel, outs, smem, held, vmem, scratch=(), out_specs=None):
    held = [pltpu.with_memory_space_constraint(value, pltpu.HBM) for value in held]
    return pl.pallas_call(
        kernel,
        out_shape=outs,
        in_specs=[SMEM] * len(smem) + [HBM] * len(held) + [VMEM] * len(vmem),
        out_specs=out_specs or [VMEM] * len(outs),
        scratch_shapes=list(scratch),
        compiler_params=pltpu.CompilerParams(vmem_limit_bytes=min(48, lax.axis_size("blk") + 8) * MIB),
    )(*smem, *held, *vmem)


def local(tiles, tile_rows, tile_cols, start_right):
    blocks = lax.axis_size("blk")
    group = lax.axis_size("rep")
    block = lax.axis_index("blk")
    tile = tiles.shape[-1]
    share, width = start_right.shape
    flat_tiles = tiles.reshape(-1, tile, tile)
    held = flat_tiles.shape[0]
    quarter = tile // group
    total_rows = ROW_TILES * tile * blocks
    total_cols = share * group * blocks
    count = blocks * group
    packed_rows = 2 * width + width // 2
    shape = jax.ShapeDtypeStruct

    def across(value):
        return lax.all_to_all(value, "blk", split_axis=0, concat_axis=0, tiled=True)

    def swap_x(value):
        return lax.ppermute(value, "rep", [(i, i ^ 2) for i in range(group)])

    def swap_core(value):
        return lax.ppermute(value, "rep", [(i, i ^ 1) for i in range(group)])

    moved, start = call(
        pack_kernel,
        [shape((count, quarter + 8, tile), BF16), shape((width, share), BF16)],
        [],
        [tile_rows, tile_cols, flat_tiles.reshape(count, quarter, tile), start_right.T],
        [],
        [
            pltpu.SMEM(tile_rows.shape, jnp.int32),
            pltpu.SMEM(tile_cols.shape, jnp.int32),
            pltpu.VMEM((count, quarter, tile), BF16),
            pltpu.VMEM((width, share), F32),
            pltpu.SemaphoreType.DMA((4,)),
        ],
    )
    start_own = jnp.stack([start, swap_x(start)])
    start_near = swap_core(start_own)
    moved = lax.all_to_all(moved, ("blk", "rep"), split_axis=0, concat_axis=0, tiled=True)
    chosen, places = call(
        choose_kernel,
        [shape((blocks, 2 * width, tile), BF16), shape((count, 8, tile), jnp.int32)],
        [],
        [],
        [moved, start_own, start_near],
        [pltpu.VMEM((blocks, 2 * width, tile), BF16), pltpu.SemaphoreType.DMA((blocks,))],
        [HBM, VMEM],
    )
    flat_tiles, moved = lax.optimization_barrier((flat_tiles, moved))
    tiles_own = jnp.stack([flat_tiles, swap_x(flat_tiles)])
    tiles_near = swap_core(tiles_own)
    columns_own = jnp.stack([moved, swap_x(moved)])
    columns_near = swap_core(columns_own)
    places = places[:, 0, 0 : 2 * held].reshape(blocks, group, 2 * held)
    rows_all = lax.dynamic_index_in_dim(places, block, 0, keepdims=False)[:, 0:held]
    cols_here = lax.dynamic_index_in_dim(places, held + block, 2, keepdims=False)

    packed = pltpu.VMEM((width, 2 * width), BF16)
    work = pltpu.VMEM((width, 2 * width), F32)
    spread = pltpu.VMEM((2, 8, 8, 2 * width), F32)
    slot_scratch = [pltpu.SMEM((blocks, group), jnp.int32), pltpu.SMEM((share * group // tile,), jnp.int32)]
    for iteration in range(ITERS):
        first, last = iteration == 0, iteration == ITERS - 1
        chosen = across(chosen)
        outs = [shape((blocks, packed_rows, tile), BF16)]
        if last:
            outs.append(shape((width, ROW_TILES * tile), F32))
        results = call(
            functools.partial(left_kernel, first, last),
            outs,
            [],
            [],
            [rows_all, tiles_own, tiles_near, chosen, swap_core(chosen)],
            [
                pltpu.VMEM((width, ROW_TILES * tile), F32),
                pltpu.VMEM((2 * width if first else width, ROW_TILES * tile), BF16),
                packed,
                work,
                spread,
                pltpu.VMEM((width, 2 * width), F32),
                pltpu.SMEM(rows_all.shape, jnp.int32),
                pltpu.SemaphoreType.DMA((1,)),
            ]
            + ([pltpu.SemaphoreType.DMA((blocks, 3))] if first else [])
            + ([pltpu.VMEM((group, blocks, width, tile), F32)] if first and blocks <= 8 else []),
            [HBM] if first else None,
        )
        picked = across(results[0])
        left_raw = results[-1]
        total = pltpu.VMEM((width, count * tile), F32)
        gram_scratch = pltpu.VMEM((width, 2 * width), F32)
        quarters = pltpu.VMEM((group, count, quarter, tile), BF16)
        other = swap_core(picked)
        if last:
            break
        (chosen,) = call(
            right_kernel,
            [shape((blocks, packed_rows, tile), BF16)],
            [],
            [],
            [cols_here, columns_own, columns_near, picked, other],
            [total, pltpu.VMEM((width, count * tile), BF16), packed, work, spread, gram_scratch, quarters]
            + [pltpu.SMEM(cols_here.shape, jnp.int32), pltpu.SemaphoreType.DMA((1,))]
            + slot_scratch,
        )
    (slots,) = call(
        slots_kernel,
        [shape(cols_here.shape, jnp.int32)],
        [cols_here],
        [],
        [],
        slot_scratch[1:],
        [SMEM],
    )
    (gram,) = call(
        last_right_kernel,
        [shape((blocks, width // 2, 2 * width), F32)],
        [],
        [],
        [slots, columns_own, columns_near, picked, other],
        [total, gram_scratch, quarters, pltpu.SMEM(slots.shape, jnp.int32), pltpu.SemaphoreType.DMA((blocks + 1,))],
        [HBM],
    )
    left, parts, left_scale = call(
        functools.partial(between_kernel, math.sqrt(total_rows), math.sqrt(total_cols)),
        [shape(left_raw.shape, F32), shape((2 * width, share), BF16), shape((width, width), F32)],
        [cols_here, slots],
        [],
        [columns_own, columns_near, picked, other, left_raw],
        [pltpu.VMEM((width, share), F32), work, spread, total, gram_scratch, quarters],
    )
    (right,) = call(
        finish_kernel,
        [shape((width, share), F32)],
        [],
        [],
        [across(gram), left_scale, parts],
        [work, spread, pltpu.VMEM((width, share), F32), pltpu.SemaphoreType.DMA((4,))],
        [HBM],
    )
    return (left.T, right.T)


def solution(mesh):
    in_specs = (
        P("blk", "rep", None, None),
        P("blk", "rep"),
        P("blk", "rep"),
        P(("blk", "rep"), None),
    )
    out_specs = (P("blk", None), P(("blk", "rep"), None))
    return jax.shard_map(local, mesh=mesh, in_specs=in_specs, out_specs=out_specs, check_vma=False)
```

```python
import functools
import math

import jax
import jax.numpy as jnp
from jax import lax
from jax.experimental import pallas as pl
from jax.experimental.pallas import tpu as pltpu
from jax.sharding import PartitionSpec as P

ITERS = 2
ROW_TILES = 16
F32 = jnp.float32
BF16 = jnp.bfloat16
MIB = 1024 * 1024
NT = (((1,), (1,)), ((), ()))
NN = (((1,), (0,)), ((), ()))


def dot(a, b, dims):
    return lax.dot_general(a, b, dims, preferred_element_type=F32)


def exact_dot(a, b):
    return lax.dot_general(a, b, NN, precision=lax.Precision.HIGHEST, preferred_element_type=F32)


def two_parts(value):
    high = value.astype(BF16)
    return high, (value - high.astype(F32)).astype(BF16)


def eliminate(work, spread):
    size = work.shape[0]
    for k in range(size // 8):
        at = size + 8 * k
        panel = work[8 * k : 8 * k + 8, :]
        shape = panel.shape
        for s in range(8):
            spread[k % 2, s] = jnp.broadcast_to(panel[:, at + s : at + s + 1], shape)
        d = {(i, s): jnp.broadcast_to(spread[k % 2, s, i : i + 1, :], shape) for s in range(8) for i in range(s, 8)}
        rows = [jnp.broadcast_to(work[8 * k + s : 8 * k + s + 1, :], shape) for s in range(8)]
        inverse = [None] * 8
        lower = {}
        for s in range(8):
            inverse[s] = 1.0 / d[s, s]
            for i in range(s + 1, 8):
                lower[i, s] = d[i, s] * inverse[s]
            for i in range(s + 1, 8):
                for j in range(s + 1, i + 1):
                    d[i, j] = d[i, j] - lower[i, s] * d[j, s]
                rows[i] = rows[i] - lower[i, s] * rows[s]
        for s in range(8):
            work[8 * k + s : 8 * k + s + 1, :] = (rows[s] * lax.rsqrt(d[s, s]))[0:1, :]
        solved = [rows[s] * inverse[s] for s in range(8)]
        below = [work[at : at + 8, :] for at in range(8 * k + 8, size, 8)]
        updated = list(below)
        for s in reversed(range(8)):
            for i in range(s):
                solved[i] = solved[i] - lower[s, i] * solved[s]
            for i, old in enumerate(below):
                updated[i] = updated[i] - jnp.broadcast_to(old[:, at + s : at + s + 1], shape) * solved[s]
        for i, new in enumerate(updated):
            work[8 * (k + 1 + i) : 8 * (k + 2 + i), :] = new
        yield


def run(steps):
    for _ in steps:
        pass


def put_identity(work):
    size = work.shape[0]
    row = lax.broadcasted_iota(jnp.int32, work.shape, 0)
    column = lax.broadcasted_iota(jnp.int32, work.shape, 1)
    work[...] = jnp.where(row == column, 1.0, 0.0).astype(F32)


def gather_gram(work, own_ref, other_ref, core):
    size = work.shape[0]
    half = size // 2
    put_identity(work)
    for source, at_core in ((own_ref, core), (other_ref, 1 - core)):
        total = jnp.zeros((half, 2 * size), F32)
        for b in range(source.shape[0]):
            total = total + source[b, 2 * size :, :].astype(F32)
        total = total + pltpu.roll(total, size, 1)
        at = pl.multiple_of(at_core * half, half)
        work[pl.ds(at, half), size:] = total[:, size:]


def gram_of_parts(parts):
    width = parts.shape[0] // 2
    full = dot(parts, parts, NT)
    full = full[0:width] + full[width:]
    return full + pltpu.roll(full, width, 1)


def apply_scale(scale_parts, value):
    high, low = two_parts(value)
    scale_high, scale_low = scale_parts
    return dot(
        jnp.concatenate([scale_high, scale_high, scale_low], axis=1),
        jnp.concatenate([high, low, high], axis=0),
        NN,
    )


def each(count, body, step=8):
    if count <= step:
        for i in range(count):
            body(i)
    else:

        def several(o, carry):
            for i in range(step):
                body(o * step + i)
            return carry

        lax.fori_loop(0, count // step, several, 0)


def beside(steps, ready, tasks):
    next(steps, None)
    ready()
    if max(count for _, count in tasks) > 8:
        run(steps)
        for body, count in tasks:
            each(count, body)
        return
    tasks = [functools.partial(body, i) for body, count in tasks for i in range(count)]
    panels = 8
    for n in range(panels):
        for task in tasks[len(tasks) * n // panels : len(tasks) * (n + 1) // panels]:
            task()
        next(steps, None)
    run(steps)


def lanes(index, size):
    return pl.ds(index * size if isinstance(index, int) else pl.multiple_of(index * size, size), size)


def add_gram(total, raw_gram, chunk):
    def add(o):
        raw_gram[...] += gram_of_parts(jnp.concatenate(two_parts(total[:, lanes(o, chunk)]), axis=0))

    return add


def scaled_gram(scale, raw_gram):
    width = scale.shape[0]
    once = exact_dot(scale, raw_gram[:, 0:width])
    return lax.dot_general(
        once,
        jnp.concatenate([scale, scale], axis=0),
        NT,
        precision=lax.Precision.HIGHEST,
        preferred_element_type=F32,
    )


def pack_kernel(
    rows_hbm, cols_hbm, tiles_hbm, start_hbm, out_ref, start_out, rows_ref, cols_ref, tiles_ref, start_ref, sems
):
    pairs = ((rows_hbm, rows_ref), (cols_hbm, cols_ref), (tiles_hbm, tiles_ref), (start_hbm, start_ref))
    copies = [pltpu.make_async_copy(source, to, sems.at[n]) for n, (source, to) in enumerate(pairs)]
    for copy in copies:
        copy.start()
    count, quarter, tile = tiles_ref.shape
    held = rows_ref.shape[1]
    lane = lax.broadcasted_iota(jnp.int32, (8, tile), 1)
    places = jnp.zeros((8, tile), jnp.int32)
    copies[0].wait()
    copies[1].wait()
    for j in range(held):
        places = jnp.where(lane == j, rows_ref[0, j], jnp.where(lane == held + j, cols_ref[0, j], places))
    places = places.astype(F32).astype(BF16)
    copies[2].wait()

    def pack(i):
        out_ref[i] = jnp.concatenate([tiles_ref[i], places], axis=0)

    each(count, pack, 32)
    copies[3].wait()
    start_out[...] = start_ref[...].astype(BF16)


def choose_kernel(moved_ref, own_ref, near_ref, out_ref, places_ref):
    rep, block = lax.axis_index("rep"), lax.axis_index("blk")
    core = lax.rem(rep, 2)
    blocks, _, tile = out_ref.shape
    width, share = own_ref.shape[1:]
    per_share = share // tile
    lane = lax.broadcasted_iota(jnp.int32, (8, tile), 1)

    def choose(b):
        for r in range(4):
            entry = moved_ref[b * 4 + r]
            entry = entry[entry.shape[0] - 8 :, :].astype(F32)
            places_ref[b * 4 + r] = entry.astype(jnp.int32)
        for x in range(2):
            entry = moved_ref[b * 4 + x * 2 + core]
            entry = entry[entry.shape[0] - 8 :, :].astype(F32)
            col = jnp.max(jnp.where(lane == blocks + block, entry, 0.0)).astype(jnp.int32)
            at = pl.multiple_of(lax.rem(col, per_share) * tile, tile)
            away = lax.bitwise_xor(lax.div(col, per_share), rep)
            far = lax.div(away, 2)
            mine = own_ref[far, :, pl.ds(at, tile)]
            theirs = near_ref[far, :, pl.ds(at, tile)]
            out_ref[b, x * width : (x + 1) * width, :] = jnp.where(lax.rem(away, 2) == 0, mine, theirs)

    each(blocks, choose)


def find_slots(cols_ref, slots_ref, first_at):
    blocks, group = cols_ref.shape

    def note(o):
        b = blocks - 1 - o
        for r in reversed(range(group)):
            first_at[cols_ref[b, r]] = b * group + r

    def look(b):
        for r in range(group):
            slots_ref[b, r] = first_at[cols_ref[b, r]]

    each(blocks, note)
    each(blocks, look)


def left_kernel(first, last, rows_vmem, tiles_own, tiles_near, own_ref, other_ref, out_ref, *rest):
    if last:
        raw_ref, *rest = rest
    total, stacked, packed, work, spread, raw_gram, rows_ref, rows_sem, *rest = rest
    rows = pltpu.make_async_copy(rows_vmem, rows_ref, rows_sem.at[0])
    rows.start()
    this = lax.axis_index("rep")
    core = lax.rem(this, 2)
    pieces, _, tile = own_ref.shape
    width = total.shape[0]
    half = width // 2
    if not first:
        gather_gram(work, own_ref, other_ref, core)
    steps = eliminate(work, spread) if not first else iter(())
    total[...] = jnp.zeros_like(total)

    early = first and pieces <= 8
    if first:
        sems, *rest = rest
    if early:
        (products,) = rest
    tasks = []
    for far in range(2):
        for source, stored, near in ((own_ref, tiles_own, 0), (other_ref, tiles_near, 1)):
            rep = lax.bitwise_xor(this, 2 * far + near)

            def multiply(p, source=source, stored=stored, far=far, rep=rep):
                chosen = source[p, pl.ds(pl.multiple_of(lax.div(rep, 2) * width, width), width), :]
                return dot(chosen, stored[far, p], NT)

            def add(p, rep=rep, multiply=multiply, kept=2 * far + near):
                product = products[kept, p] if early else multiply(p)
                at = pl.multiple_of(rows_ref[rep, p] * tile, tile)
                total[:, pl.ds(at, tile)] += product

            tasks.append((add, pieces))
            if early:
                for p in range(pieces):
                    products[2 * far + near, p] = multiply(p)
    chunk = 4 * tile
    if not first:
        raw_gram[...] = jnp.zeros_like(raw_gram)
        tasks.append((add_gram(total, raw_gram, chunk), total.shape[1] // chunk))
    beside(steps, rows.wait, tasks)
    mine = pl.ds(pl.multiple_of(core * half, half), half)
    if first:
        stacked[...] = jnp.concatenate(two_parts(total[...]), axis=0)
        copies = []
        for p in range(pieces):
            for x in range(2):
                at = pl.multiple_of(rows_ref[x * 2 + core, p] * tile, tile)
                copies.append(
                    pltpu.make_async_copy(
                        stacked.at[pl.ds(0, width), pl.ds(at, tile)],
                        out_ref.at[p, pl.ds(x * width, width), :],
                        sems.at[p, x],
                    )
                )
                copies[-1].start()
        pack_gram(gram_of_parts(stacked[...]), packed)
        for p in range(pieces):
            copies.append(
                pltpu.make_async_copy(packed.at[mine, :], out_ref.at[p, pl.ds(2 * width, half), :], sems.at[p, 2])
            )
            copies[-1].start()
        for copy in copies:
            copy.wait()
        return
    scale = work[:, 0:width]
    pack_gram(scaled_gram(scale, raw_gram), packed)
    scale = two_parts(scale)

    def apply(o):
        at = lanes(o, chunk)
        value = apply_scale(scale, total[:, at])
        if last:
            raw_ref[:, at] = value
        stacked[0:width, at] = value.astype(BF16)

    each(total.shape[1] // chunk, apply)
    mine = packed[mine, :]

    def send(p):
        for x in range(2):
            at = pl.multiple_of(rows_ref[x * 2 + core, p] * tile, tile)
            out_ref[p, x * width : (x + 1) * width, :] = stacked[0:width, pl.ds(at, tile)]
        out_ref[p, 2 * width :, :] = mine

    each(pieces, send)


def pack_gram(gram_twice, packed):
    high, low = two_parts(gram_twice)
    lane = lax.broadcasted_iota(jnp.int32, gram_twice.shape, 1)
    packed[...] = jnp.where(lane < gram_twice.shape[0], high.astype(F32), low.astype(F32)).astype(BF16)


def slots_kernel(cols_ref, slots_ref, first_at):
    find_slots(cols_ref, slots_ref, first_at)


def place_quarters(tiles_own, tiles_near, quarters):
    quarter = quarters.shape[2]
    for far in range(2):
        for near, source in enumerate((tiles_own, tiles_near)):
            quarters[lax.bitwise_xor(lax.axis_index("rep"), 2 * far + near)] = source[far, :, 0:quarter, :]


def right_tasks(slots_ref, quarters, own_ref, other_ref, total, raw_gram):
    core = lax.rem(lax.axis_index("rep"), 2)
    blocks, _, tile = own_ref.shape
    width = total.shape[0]
    total[...] = jnp.zeros_like(total)
    raw_gram[...] = jnp.zeros_like(raw_gram)
    tasks = []
    for x in range(2):
        for source, at_core in ((own_ref, core), (other_ref, 1 - core)):

            def add(b, source=source, x=x, rep=x * 2 + at_core):
                stored = jnp.concatenate([quarters[q, b * 4 + rep] for q in range(4)], axis=0)
                product = dot(source[b, x * width : (x + 1) * width, :], stored, NN)
                at = pl.multiple_of(slots_ref[b, rep] * tile, tile)
                total[:, pl.ds(at, tile)] += product

            tasks.append((add, blocks))
    chunk = 8 * tile
    tasks.append((add_gram(total, raw_gram, chunk), total.shape[1] // chunk))
    return tasks


def right_kernel(
    cols_vmem,
    tiles_own,
    tiles_near,
    own_ref,
    other_ref,
    out_ref,
    total,
    stacked,
    packed,
    work,
    spread,
    raw_gram,
    quarters,
    cols_ref,
    cols_sem,
    slots_ref,
    first_at,
):
    cols = pltpu.make_async_copy(cols_vmem, cols_ref, cols_sem.at[0])
    cols.start()
    core = lax.rem(lax.axis_index("rep"), 2)
    blocks, _, tile = own_ref.shape
    width = total.shape[0]
    half = width // 2
    place_quarters(tiles_own, tiles_near, quarters)
    gather_gram(work, own_ref, other_ref, core)

    def ready():
        cols.wait()
        find_slots(cols_ref, slots_ref, first_at)

    tasks = right_tasks(slots_ref, quarters, own_ref, other_ref, total, raw_gram)
    beside(eliminate(work, spread), ready, tasks)
    scale = work[:, 0:width]
    pack_gram(scaled_gram(scale, raw_gram), packed)
    scale_parts = two_parts(scale)
    chunk = 8 * tile

    def apply(o):
        at = lanes(o, chunk)
        stacked[0:width, at] = apply_scale(scale_parts, total[:, at]).astype(BF16)

    each(total.shape[1] // chunk, apply)
    mine = packed[pl.ds(pl.multiple_of(core * half, half), half), :]

    def send(b):
        for x in range(2):
            at = pl.multiple_of(slots_ref[b, x * 2 + core] * tile, tile)
            out_ref[b, x * width : (x + 1) * width, :] = stacked[0:width, pl.ds(at, tile)]
        out_ref[b, 2 * width :, :] = mine

    each(blocks, send)


def last_right_kernel(
    slots_vmem, tiles_own, tiles_near, own_ref, other_ref, gram_hbm, total, raw_gram, quarters, slots_ref, sems
):
    slots = pltpu.make_async_copy(slots_vmem, slots_ref, sems.at[gram_hbm.shape[0]])
    slots.start()
    place_quarters(tiles_own, tiles_near, quarters)
    tasks = right_tasks(slots_ref, quarters, own_ref, other_ref, total, raw_gram)
    beside(iter(()), slots.wait, tasks)
    width = total.shape[0]
    half = width // 2
    lane = lax.broadcasted_iota(jnp.int32, (half, 2 * width), 1)
    raw_gram[0:half, :] = jnp.where(lane < width, raw_gram[0:half, :], raw_gram[half:, :])
    copies = [
        pltpu.make_async_copy(raw_gram.at[pl.ds(0, half), :], gram_hbm.at[b], sems.at[b])
        for b in range(gram_hbm.shape[0])
    ]
    for copy in copies:
        copy.start()
    for copy in copies:
        copy.wait()


def between_kernel(
    left_factor,
    right_factor,
    cols_ref,
    slots_ref,
    tiles_own,
    tiles_near,
    own_ref,
    other_ref,
    left_ref,
    left_out,
    parts_ref,
    scale_ref,
    share,
    work,
    spread,
    total_ref,
    raw_gram,
    quarters,
):
    place_quarters(tiles_own, tiles_near, quarters)
    gather_gram(work, own_ref, other_ref, lax.rem(lax.axis_index("rep"), 2))
    products = right_tasks(slots_ref, quarters, own_ref, other_ref, total_ref, raw_gram)[:-1]
    beside(eliminate(work, spread), lambda: None, products)
    scale_ref[...] = work[:, 0 : scale_ref.shape[1]]
    left_out[...] = exact_dot(scale_ref[...] * left_factor, left_ref[...])
    width, tile = share.shape[0], total_ref.shape[1] // (slots_ref.shape[0] * 4)
    shares = share.shape[1] // tile
    share[...] = jnp.zeros_like(share)

    def keep(b):
        for rep in range(4):
            col = cols_ref[b, rep]

            @pl.when(lax.div(col, shares) == lax.axis_index("rep"))
            def _():
                to = pl.multiple_of(lax.rem(col, shares) * tile, tile)
                at = pl.multiple_of(slots_ref[b, rep] * tile, tile)
                share[:, pl.ds(to, tile)] = total_ref[:, pl.ds(at, tile)]

    each(slots_ref.shape[0], keep)
    for n, part in enumerate(two_parts(apply_scale(two_parts(scale_ref[...] * right_factor), share[...]))):
        parts_ref[n * width : (n + 1) * width, :] = part


def finish_kernel(gram_ref, scale_ref, parts_ref, right_hbm, work, spread, right, sems):
    width = scale_ref.shape[0]
    half = width // 2
    total = gram_ref[0]
    for b in range(1, gram_ref.shape[0]):
        total = total + gram_ref[b]
    gram = scaled_gram(scale_ref[...], jnp.concatenate([total[:, 0:width], total[:, width:]], axis=0))
    put_identity(work)
    work[:, width:] = gram[:, width:]
    run(eliminate(work, spread))
    high, low = two_parts(work[:, 0:width])
    scale = jnp.concatenate([high, high], axis=1)
    chunk = right.shape[1] // 4
    copies = []
    for n in range(4):
        at = pl.ds(n * chunk, chunk)
        right[:, at] = dot(scale, parts_ref[:, at], NN) + dot(low, parts_ref[0:width, at], NN)
        copies.append(pltpu.make_async_copy(right.at[:, at], right_hbm.at[:, at], sems.at[n]))
        copies[-1].start()
    for copy in copies:
        copy.wait()


SMEM = pl.BlockSpec(memory_space=pltpu.SMEM)
VMEM = pl.BlockSpec(memory_space=pltpu.VMEM)
HBM = pl.BlockSpec(memory_space=pltpu.HBM)


def call(kernel, outs, smem, held, vmem, scratch=(), out_specs=None):
    held = [pltpu.with_memory_space_constraint(value, pltpu.HBM) for value in held]
    return pl.pallas_call(
        kernel,
        out_shape=outs,
        in_specs=[SMEM] * len(smem) + [HBM] * len(held) + [VMEM] * len(vmem),
        out_specs=out_specs or [VMEM] * len(outs),
        scratch_shapes=list(scratch),
        compiler_params=pltpu.CompilerParams(vmem_limit_bytes=min(48, lax.axis_size("blk") + 8) * MIB),
    )(*smem, *held, *vmem)


def local(tiles, tile_rows, tile_cols, start_right):
    blocks = lax.axis_size("blk")
    group = lax.axis_size("rep")
    block = lax.axis_index("blk")
    tile = tiles.shape[-1]
    share, width = start_right.shape
    flat_tiles = tiles.reshape(-1, tile, tile)
    held = flat_tiles.shape[0]
    quarter = tile // group
    total_rows = ROW_TILES * tile * blocks
    total_cols = share * group * blocks
    count = blocks * group
    packed_rows = 2 * width + width // 2
    shape = jax.ShapeDtypeStruct

    def across(value):
        return lax.all_to_all(value, "blk", split_axis=0, concat_axis=0, tiled=True)

    def swap_x(value):
        return lax.ppermute(value, "rep", [(i, i ^ 2) for i in range(group)])

    def swap_core(value):
        return lax.ppermute(value, "rep", [(i, i ^ 1) for i in range(group)])

    moved, start = call(
        pack_kernel,
        [shape((count, quarter + 8, tile), BF16), shape((width, share), BF16)],
        [],
        [tile_rows, tile_cols, flat_tiles.reshape(count, quarter, tile), start_right.T],
        [],
        [
            pltpu.SMEM(tile_rows.shape, jnp.int32),
            pltpu.SMEM(tile_cols.shape, jnp.int32),
            pltpu.VMEM((count, quarter, tile), BF16),
            pltpu.VMEM((width, share), F32),
            pltpu.SemaphoreType.DMA((4,)),
        ],
    )
    start_own = jnp.stack([start, swap_x(start)])
    start_near = swap_core(start_own)
    moved = lax.all_to_all(moved, ("blk", "rep"), split_axis=0, concat_axis=0, tiled=True)
    chosen, places = call(
        choose_kernel,
        [shape((blocks, 2 * width, tile), BF16), shape((count, 8, tile), jnp.int32)],
        [],
        [],
        [moved, start_own, start_near],
    )
    flat_tiles, moved = lax.optimization_barrier((flat_tiles, moved))
    tiles_own = jnp.stack([flat_tiles, swap_x(flat_tiles)])
    tiles_near = swap_core(tiles_own)
    columns_own = jnp.stack([moved, swap_x(moved)])
    columns_near = swap_core(columns_own)
    places = places[:, 0, 0 : 2 * held].reshape(blocks, group, 2 * held)
    rows_all = lax.dynamic_index_in_dim(places, block, 0, keepdims=False)[:, 0:held]
    cols_here = lax.dynamic_index_in_dim(places, held + block, 2, keepdims=False)

    packed = pltpu.VMEM((width, 2 * width), BF16)
    work = pltpu.VMEM((width, 2 * width), F32)
    spread = pltpu.VMEM((2, 8, 8, 2 * width), F32)
    slot_scratch = [pltpu.SMEM((blocks, group), jnp.int32), pltpu.SMEM((share * group // tile,), jnp.int32)]
    for iteration in range(ITERS):
        first, last = iteration == 0, iteration == ITERS - 1
        chosen = across(chosen)
        outs = [shape((blocks, packed_rows, tile), BF16)]
        if last:
            outs.append(shape((width, ROW_TILES * tile), F32))
        results = call(
            functools.partial(left_kernel, first, last),
            outs,
            [],
            [],
            [rows_all, tiles_own, tiles_near, chosen, swap_core(chosen)],
            [
                pltpu.VMEM((width, ROW_TILES * tile), F32),
                pltpu.VMEM((2 * width if first else width, ROW_TILES * tile), BF16),
                packed,
                work,
                spread,
                pltpu.VMEM((width, 2 * width), F32),
                pltpu.SMEM(rows_all.shape, jnp.int32),
                pltpu.SemaphoreType.DMA((1,)),
            ]
            + ([pltpu.SemaphoreType.DMA((blocks, 3))] if first else [])
            + ([pltpu.VMEM((group, blocks, width, tile), F32)] if first and blocks <= 8 else []),
            [HBM] if first else None,
        )
        picked = across(results[0])
        left_raw = results[-1]
        total = pltpu.VMEM((width, count * tile), F32)
        gram_scratch = pltpu.VMEM((width, 2 * width), F32)
        quarters = pltpu.VMEM((group, count, quarter, tile), BF16)
        other = swap_core(picked)
        if last:
            break
        (chosen,) = call(
            right_kernel,
            [shape((blocks, packed_rows, tile), BF16)],
            [],
            [],
            [cols_here, columns_own, columns_near, picked, other],
            [total, pltpu.VMEM((width, count * tile), BF16), packed, work, spread, gram_scratch, quarters]
            + [pltpu.SMEM(cols_here.shape, jnp.int32), pltpu.SemaphoreType.DMA((1,))]
            + slot_scratch,
        )
    (slots,) = call(
        slots_kernel,
        [shape(cols_here.shape, jnp.int32)],
        [cols_here],
        [],
        [],
        slot_scratch[1:],
        [SMEM],
    )
    (gram,) = call(
        last_right_kernel,
        [shape((blocks, width // 2, 2 * width), F32)],
        [],
        [],
        [slots, columns_own, columns_near, picked, other],
        [total, gram_scratch, quarters, pltpu.SMEM(slots.shape, jnp.int32), pltpu.SemaphoreType.DMA((blocks + 1,))],
        [HBM],
    )
    left, parts, left_scale = call(
        functools.partial(between_kernel, math.sqrt(total_rows), math.sqrt(total_cols)),
        [shape(left_raw.shape, F32), shape((2 * width, share), BF16), shape((width, width), F32)],
        [cols_here, slots],
        [],
        [columns_own, columns_near, picked, other, left_raw],
        [pltpu.VMEM((width, share), F32), work, spread, total, gram_scratch, quarters],
    )
    (right,) = call(
        finish_kernel,
        [shape((width, share), F32)],
        [],
        [],
        [across(gram), left_scale, parts],
        [work, spread, pltpu.VMEM((width, share), F32), pltpu.SemaphoreType.DMA((4,))],
        [HBM],
    )
    return (left.T, right.T)


def solution(mesh):
    in_specs = (
        P("blk", "rep", None, None),
        P("blk", "rep"),
        P("blk", "rep"),
        P(("blk", "rep"), None),
    )
    out_specs = (P("blk", None), P(("blk", "rep"), None))
    return jax.shard_map(local, mesh=mesh, in_specs=in_specs, out_specs=out_specs, check_vma=False)
```

```python
import functools
import math

import jax
import jax.numpy as jnp
from jax import lax
from jax.experimental import pallas as pl
from jax.experimental.pallas import tpu as pltpu
from jax.sharding import PartitionSpec as P

ITERS = 2
ROW_TILES = 16
F32 = jnp.float32
BF16 = jnp.bfloat16
MIB = 1024 * 1024
NT = (((1,), (1,)), ((), ()))
NN = (((1,), (0,)), ((), ()))


def dot(a, b, dims):
    return lax.dot_general(a, b, dims, preferred_element_type=F32)


def exact_dot(a, b):
    return lax.dot_general(a, b, NN, precision=lax.Precision.HIGHEST, preferred_element_type=F32)


def two_parts(value):
    high = value.astype(BF16)
    return high, (value - high.astype(F32)).astype(BF16)


def eliminate(work, spread):
    size = work.shape[0]
    for k in range(size // 8):
        at = size + 8 * k
        panel = work[8 * k : 8 * k + 8, :]
        shape = panel.shape
        for s in range(8):
            spread[k % 2, s] = jnp.broadcast_to(panel[:, at + s : at + s + 1], shape)
        d = {(i, s): jnp.broadcast_to(spread[k % 2, s, i : i + 1, :], shape) for s in range(8) for i in range(s, 8)}
        rows = [jnp.broadcast_to(work[8 * k + s : 8 * k + s + 1, :], shape) for s in range(8)]
        inverse = [None] * 8
        lower = {}
        for s in range(8):
            inverse[s] = 1.0 / d[s, s]
            for i in range(s + 1, 8):
                lower[i, s] = d[i, s] * inverse[s]
            for i in range(s + 1, 8):
                for j in range(s + 1, i + 1):
                    d[i, j] = d[i, j] - lower[i, s] * d[j, s]
                rows[i] = rows[i] - lower[i, s] * rows[s]
        for s in range(8):
            work[8 * k + s : 8 * k + s + 1, :] = (rows[s] * lax.rsqrt(d[s, s]))[0:1, :]
        solved = [rows[s] * inverse[s] for s in range(8)]
        below = [work[at : at + 8, :] for at in range(8 * k + 8, size, 8)]
        updated = list(below)
        for s in reversed(range(8)):
            for i in range(s):
                solved[i] = solved[i] - lower[s, i] * solved[s]
            for i, old in enumerate(below):
                updated[i] = updated[i] - jnp.broadcast_to(old[:, at + s : at + s + 1], shape) * solved[s]
        for i, new in enumerate(updated):
            work[8 * (k + 1 + i) : 8 * (k + 2 + i), :] = new
        yield


def run(steps):
    for _ in steps:
        pass


def put_identity(work):
    size = work.shape[0]
    row = lax.broadcasted_iota(jnp.int32, work.shape, 0)
    column = lax.broadcasted_iota(jnp.int32, work.shape, 1)
    work[...] = jnp.where(row == column, 1.0, 0.0).astype(F32)


def gather_gram(work, own_ref, other_ref, core):
    size = work.shape[0]
    half = size // 2
    put_identity(work)
    for source, at_core in ((own_ref, core), (other_ref, 1 - core)):
        total = jnp.zeros((half, 2 * size), F32)
        for b in range(source.shape[0]):
            total = total + source[b, 2 * size :, :].astype(F32)
        total = total + pltpu.roll(total, size, 1)
        at = pl.multiple_of(at_core * half, half)
        work[pl.ds(at, half), size:] = total[:, size:]


def gram_of_parts(parts):
    width = parts.shape[0] // 2
    full = dot(parts, parts, NT)
    full = full[0:width] + full[width:]
    return full + pltpu.roll(full, width, 1)


def apply_scale(scale_parts, value):
    high, low = two_parts(value)
    scale_high, scale_low = scale_parts
    return dot(
        jnp.concatenate([scale_high, scale_high, scale_low], axis=1),
        jnp.concatenate([high, low, high], axis=0),
        NN,
    )


def each(count, body, step=8):
    if count <= step:
        for i in range(count):
            body(i)
    else:

        def several(o, carry):
            for i in range(step):
                body(o * step + i)
            return carry

        lax.fori_loop(0, count // step, several, 0)


def beside(steps, ready, tasks):
    next(steps, None)
    ready()
    if max(count for _, count in tasks) > 8:
        run(steps)
        for body, count in tasks:
            each(count, body)
        return
    tasks = [functools.partial(body, i) for body, count in tasks for i in range(count)]
    panels = 8
    for n in range(panels):
        for task in tasks[len(tasks) * n // panels : len(tasks) * (n + 1) // panels]:
            task()
        next(steps, None)
    run(steps)


def lanes(index, size):
    return pl.ds(index * size if isinstance(index, int) else pl.multiple_of(index * size, size), size)


def add_gram(total, raw_gram, chunk):
    def add(o):
        raw_gram[...] += gram_of_parts(jnp.concatenate(two_parts(total[:, lanes(o, chunk)]), axis=0))

    return add


def scaled_gram(scale, raw_gram):
    width = scale.shape[0]
    once = exact_dot(scale, raw_gram[:, 0:width])
    return lax.dot_general(
        once,
        jnp.concatenate([scale, scale], axis=0),
        NT,
        precision=lax.Precision.HIGHEST,
        preferred_element_type=F32,
    )


def pack_kernel(
    rows_hbm, cols_hbm, tiles_hbm, start_hbm, out_ref, start_out, rows_ref, cols_ref, tiles_ref, start_ref, sems
):
    pairs = ((rows_hbm, rows_ref), (cols_hbm, cols_ref), (tiles_hbm, tiles_ref), (start_hbm, start_ref))
    copies = [pltpu.make_async_copy(source, to, sems.at[n]) for n, (source, to) in enumerate(pairs)]
    for copy in copies:
        copy.start()
    count, quarter, tile = tiles_ref.shape
    held = rows_ref.shape[1]
    lane = lax.broadcasted_iota(jnp.int32, (8, tile), 1)
    places = jnp.zeros((8, tile), jnp.int32)
    copies[0].wait()
    copies[1].wait()
    for j in range(held):
        places = jnp.where(lane == j, rows_ref[0, j], jnp.where(lane == held + j, cols_ref[0, j], places))
    places = places.astype(F32).astype(BF16)
    copies[2].wait()

    def pack(i):
        out_ref[i] = jnp.concatenate([tiles_ref[i], places], axis=0)

    each(count, pack, 32)
    copies[3].wait()
    start_out[...] = start_ref[...].astype(BF16)


def choose_kernel(moved_ref, own_ref, near_ref, out_ref, places_ref):
    rep, block = lax.axis_index("rep"), lax.axis_index("blk")
    core = lax.rem(rep, 2)
    blocks, _, tile = out_ref.shape
    width, share = own_ref.shape[1:]
    per_share = share // tile
    lane = lax.broadcasted_iota(jnp.int32, (8, tile), 1)

    def choose(b):
        for r in range(4):
            entry = moved_ref[b * 4 + r]
            entry = entry[entry.shape[0] - 8 :, :].astype(F32)
            places_ref[b * 4 + r] = entry.astype(jnp.int32)
        for x in range(2):
            entry = moved_ref[b * 4 + x * 2 + core]
            entry = entry[entry.shape[0] - 8 :, :].astype(F32)
            col = jnp.max(jnp.where(lane == blocks + block, entry, 0.0)).astype(jnp.int32)
            at = pl.multiple_of(lax.rem(col, per_share) * tile, tile)
            away = lax.bitwise_xor(lax.div(col, per_share), rep)
            far = lax.div(away, 2)
            mine = own_ref[far, :, pl.ds(at, tile)]
            theirs = near_ref[far, :, pl.ds(at, tile)]
            out_ref[b, x * width : (x + 1) * width, :] = jnp.where(lax.rem(away, 2) == 0, mine, theirs)

    each(blocks, choose)


def find_slots(cols_ref, slots_ref, first_at):
    blocks, group = cols_ref.shape

    def note(o):
        b = blocks - 1 - o
        for r in reversed(range(group)):
            first_at[cols_ref[b, r]] = b * group + r

    def look(b):
        for r in range(group):
            slots_ref[b, r] = first_at[cols_ref[b, r]]

    each(blocks, note)
    each(blocks, look)


def left_kernel(first, last, rows_vmem, tiles_own, tiles_near, own_ref, other_ref, out_ref, *rest):
    if last:
        raw_ref, *rest = rest
    total, stacked, packed, work, spread, raw_gram, rows_ref, rows_sem, *rest = rest
    rows = pltpu.make_async_copy(rows_vmem, rows_ref, rows_sem.at[0])
    rows.start()
    this = lax.axis_index("rep")
    core = lax.rem(this, 2)
    pieces, _, tile = own_ref.shape
    width = total.shape[0]
    half = width // 2
    if not first:
        gather_gram(work, own_ref, other_ref, core)
    steps = eliminate(work, spread) if not first else iter(())
    total[...] = jnp.zeros_like(total)

    early = first and pieces <= 8
    if first:
        sems, *rest = rest
    if early:
        (products,) = rest
    tasks = []
    for far in range(2):
        for source, stored, near in ((own_ref, tiles_own, 0), (other_ref, tiles_near, 1)):
            rep = lax.bitwise_xor(this, 2 * far + near)

            def multiply(p, source=source, stored=stored, far=far, rep=rep):
                chosen = source[p, pl.ds(pl.multiple_of(lax.div(rep, 2) * width, width), width), :]
                return dot(chosen, stored[far, p], NT)

            def add(p, rep=rep, multiply=multiply, kept=2 * far + near):
                product = products[kept, p] if early else multiply(p)
                at = pl.multiple_of(rows_ref[rep, p] * tile, tile)
                total[:, pl.ds(at, tile)] += product

            tasks.append((add, pieces))
            if early:
                for p in range(pieces):
                    products[2 * far + near, p] = multiply(p)
    chunk = 4 * tile
    if not first:
        raw_gram[...] = jnp.zeros_like(raw_gram)
        tasks.append((add_gram(total, raw_gram, chunk), total.shape[1] // chunk))
    beside(steps, rows.wait, tasks)
    mine = pl.ds(pl.multiple_of(core * half, half), half)
    if first:
        stacked[...] = jnp.concatenate(two_parts(total[...]), axis=0)
        copies = []
        for p in range(pieces):
            for x in range(2):
                at = pl.multiple_of(rows_ref[x * 2 + core, p] * tile, tile)
                copies.append(
                    pltpu.make_async_copy(
                        stacked.at[pl.ds(0, width), pl.ds(at, tile)],
                        out_ref.at[p, pl.ds(x * width, width), :],
                        sems.at[p, x],
                    )
                )
                copies[-1].start()
        pack_gram(gram_of_parts(stacked[...]), packed)
        for p in range(pieces):
            copies.append(
                pltpu.make_async_copy(packed.at[mine, :], out_ref.at[p, pl.ds(2 * width, half), :], sems.at[p, 2])
            )
            copies[-1].start()
        for copy in copies:
            copy.wait()
        return
    scale = work[:, 0:width]
    pack_gram(scaled_gram(scale, raw_gram), packed)
    scale = two_parts(scale)

    def apply(o):
        at = lanes(o, chunk)
        value = apply_scale(scale, total[:, at])
        if last:
            raw_ref[:, at] = value
        stacked[0:width, at] = value.astype(BF16)

    each(total.shape[1] // chunk, apply)
    mine = packed[mine, :]

    def send(p):
        for x in range(2):
            at = pl.multiple_of(rows_ref[x * 2 + core, p] * tile, tile)
            out_ref[p, x * width : (x + 1) * width, :] = stacked[0:width, pl.ds(at, tile)]
        out_ref[p, 2 * width :, :] = mine

    each(pieces, send)


def pack_gram(gram_twice, packed):
    high, low = two_parts(gram_twice)
    lane = lax.broadcasted_iota(jnp.int32, gram_twice.shape, 1)
    packed[...] = jnp.where(lane < gram_twice.shape[0], high.astype(F32), low.astype(F32)).astype(BF16)


def slots_kernel(cols_ref, slots_ref, first_at):
    find_slots(cols_ref, slots_ref, first_at)


def place_quarters(tiles_own, tiles_near, quarters):
    quarter = quarters.shape[2]
    for far in range(2):
        for near, source in enumerate((tiles_own, tiles_near)):
            quarters[lax.bitwise_xor(lax.axis_index("rep"), 2 * far + near)] = source[far, :, 0:quarter, :]


def right_tasks(slots_ref, quarters, own_ref, other_ref, total, raw_gram):
    core = lax.rem(lax.axis_index("rep"), 2)
    blocks, _, tile = own_ref.shape
    width = total.shape[0]
    total[...] = jnp.zeros_like(total)
    raw_gram[...] = jnp.zeros_like(raw_gram)
    tasks = []
    for x in range(2):
        for source, at_core in ((own_ref, core), (other_ref, 1 - core)):

            def add(b, source=source, x=x, rep=x * 2 + at_core):
                stored = jnp.concatenate([quarters[q, b * 4 + rep] for q in range(4)], axis=0)
                product = dot(source[b, x * width : (x + 1) * width, :], stored, NN)
                at = pl.multiple_of(slots_ref[b, rep] * tile, tile)
                total[:, pl.ds(at, tile)] += product

            tasks.append((add, blocks))
    chunk = 8 * tile
    tasks.append((add_gram(total, raw_gram, chunk), total.shape[1] // chunk))
    return tasks


def right_kernel(
    cols_vmem,
    tiles_own,
    tiles_near,
    own_ref,
    other_ref,
    out_ref,
    total,
    stacked,
    packed,
    work,
    spread,
    raw_gram,
    quarters,
    cols_ref,
    cols_sem,
    slots_ref,
    first_at,
):
    cols = pltpu.make_async_copy(cols_vmem, cols_ref, cols_sem.at[0])
    cols.start()
    core = lax.rem(lax.axis_index("rep"), 2)
    blocks, _, tile = own_ref.shape
    width = total.shape[0]
    half = width // 2
    place_quarters(tiles_own, tiles_near, quarters)
    gather_gram(work, own_ref, other_ref, core)

    def ready():
        cols.wait()
        find_slots(cols_ref, slots_ref, first_at)

    tasks = right_tasks(slots_ref, quarters, own_ref, other_ref, total, raw_gram)
    beside(eliminate(work, spread), ready, tasks)
    scale = work[:, 0:width]
    pack_gram(scaled_gram(scale, raw_gram), packed)
    scale_parts = two_parts(scale)
    chunk = 8 * tile

    def apply(o):
        at = lanes(o, chunk)
        stacked[0:width, at] = apply_scale(scale_parts, total[:, at]).astype(BF16)

    each(total.shape[1] // chunk, apply)
    mine = packed[pl.ds(pl.multiple_of(core * half, half), half), :]

    def send(b):
        for x in range(2):
            at = pl.multiple_of(slots_ref[b, x * 2 + core] * tile, tile)
            out_ref[b, x * width : (x + 1) * width, :] = stacked[0:width, pl.ds(at, tile)]
        out_ref[b, 2 * width :, :] = mine

    each(blocks, send)


def last_right_kernel(
    slots_vmem, tiles_own, tiles_near, own_ref, other_ref, gram_hbm, total, raw_gram, quarters, slots_ref, sems
):
    slots = pltpu.make_async_copy(slots_vmem, slots_ref, sems.at[gram_hbm.shape[0]])
    slots.start()
    place_quarters(tiles_own, tiles_near, quarters)
    tasks = right_tasks(slots_ref, quarters, own_ref, other_ref, total, raw_gram)
    beside(iter(()), slots.wait, tasks)
    width = total.shape[0]
    half = width // 2
    lane = lax.broadcasted_iota(jnp.int32, (half, 2 * width), 1)
    raw_gram[0:half, :] = jnp.where(lane < width, raw_gram[0:half, :], raw_gram[half:, :])
    copies = [
        pltpu.make_async_copy(raw_gram.at[pl.ds(0, half), :], gram_hbm.at[b], sems.at[b])
        for b in range(gram_hbm.shape[0])
    ]
    for copy in copies:
        copy.start()
    for copy in copies:
        copy.wait()


def between_kernel(
    left_factor,
    right_factor,
    cols_ref,
    slots_ref,
    tiles_own,
    tiles_near,
    own_ref,
    other_ref,
    left_ref,
    left_out,
    parts_ref,
    scale_ref,
    share,
    work,
    spread,
    total_ref,
    raw_gram,
    quarters,
):
    place_quarters(tiles_own, tiles_near, quarters)
    gather_gram(work, own_ref, other_ref, lax.rem(lax.axis_index("rep"), 2))
    products = right_tasks(slots_ref, quarters, own_ref, other_ref, total_ref, raw_gram)[:-1]
    beside(eliminate(work, spread), lambda: None, products)
    scale_ref[...] = work[:, 0 : scale_ref.shape[1]]
    left_out[...] = exact_dot(scale_ref[...] * left_factor, left_ref[...])
    width, tile = share.shape[0], total_ref.shape[1] // (slots_ref.shape[0] * 4)
    shares = share.shape[1] // tile
    share[...] = jnp.zeros_like(share)

    def keep(b):
        for rep in range(4):
            col = cols_ref[b, rep]

            @pl.when(lax.div(col, shares) == lax.axis_index("rep"))
            def _():
                to = pl.multiple_of(lax.rem(col, shares) * tile, tile)
                at = pl.multiple_of(slots_ref[b, rep] * tile, tile)
                share[:, pl.ds(to, tile)] = total_ref[:, pl.ds(at, tile)]

    each(slots_ref.shape[0], keep)
    for n, part in enumerate(two_parts(apply_scale(two_parts(scale_ref[...] * right_factor), share[...]))):
        parts_ref[n * width : (n + 1) * width, :] = part


def finish_kernel(gram_ref, scale_ref, parts_ref, right_hbm, work, spread, right, sems):
    width = scale_ref.shape[0]
    half = width // 2
    total = gram_ref[0]
    for b in range(1, gram_ref.shape[0]):
        total = total + gram_ref[b]
    gram = scaled_gram(scale_ref[...], jnp.concatenate([total[:, 0:width], total[:, width:]], axis=0))
    put_identity(work)
    work[:, width:] = gram[:, width:]
    run(eliminate(work, spread))
    high, low = two_parts(work[:, 0:width])
    scale = jnp.concatenate([high, high], axis=1)
    chunk = right.shape[1] // 8
    copies = []
    for n in range(8):
        at = pl.ds(n * chunk, chunk)
        right[:, at] = dot(scale, parts_ref[:, at], NN) + dot(low, parts_ref[0:width, at], NN)
        copies.append(pltpu.make_async_copy(right.at[:, at], right_hbm.at[:, at], sems.at[n]))
        copies[-1].start()
    for copy in copies:
        copy.wait()


SMEM = pl.BlockSpec(memory_space=pltpu.SMEM)
VMEM = pl.BlockSpec(memory_space=pltpu.VMEM)
HBM = pl.BlockSpec(memory_space=pltpu.HBM)


def call(kernel, outs, smem, held, vmem, scratch=(), out_specs=None):
    held = [pltpu.with_memory_space_constraint(value, pltpu.HBM) for value in held]
    return pl.pallas_call(
        kernel,
        out_shape=outs,
        in_specs=[SMEM] * len(smem) + [HBM] * len(held) + [VMEM] * len(vmem),
        out_specs=out_specs or [VMEM] * len(outs),
        scratch_shapes=list(scratch),
        compiler_params=pltpu.CompilerParams(vmem_limit_bytes=min(48, lax.axis_size("blk") + 8) * MIB),
    )(*smem, *held, *vmem)


def local(tiles, tile_rows, tile_cols, start_right):
    blocks = lax.axis_size("blk")
    group = lax.axis_size("rep")
    block = lax.axis_index("blk")
    tile = tiles.shape[-1]
    share, width = start_right.shape
    flat_tiles = tiles.reshape(-1, tile, tile)
    held = flat_tiles.shape[0]
    quarter = tile // group
    total_rows = ROW_TILES * tile * blocks
    total_cols = share * group * blocks
    count = blocks * group
    packed_rows = 2 * width + width // 2
    shape = jax.ShapeDtypeStruct

    def across(value):
        return lax.all_to_all(value, "blk", split_axis=0, concat_axis=0, tiled=True)

    def swap_x(value):
        return lax.ppermute(value, "rep", [(i, i ^ 2) for i in range(group)])

    def swap_core(value):
        return lax.ppermute(value, "rep", [(i, i ^ 1) for i in range(group)])

    moved, start = call(
        pack_kernel,
        [shape((count, quarter + 8, tile), BF16), shape((width, share), BF16)],
        [],
        [tile_rows, tile_cols, flat_tiles.reshape(count, quarter, tile), start_right.T],
        [],
        [
            pltpu.SMEM(tile_rows.shape, jnp.int32),
            pltpu.SMEM(tile_cols.shape, jnp.int32),
            pltpu.VMEM((count, quarter, tile), BF16),
            pltpu.VMEM((width, share), F32),
            pltpu.SemaphoreType.DMA((4,)),
        ],
    )
    start_own = jnp.stack([start, swap_x(start)])
    start_near = swap_core(start_own)
    moved = lax.all_to_all(moved, ("blk", "rep"), split_axis=0, concat_axis=0, tiled=True)
    chosen, places = call(
        choose_kernel,
        [shape((blocks, 2 * width, tile), BF16), shape((count, 8, tile), jnp.int32)],
        [],
        [],
        [moved, start_own, start_near],
    )
    flat_tiles, moved = lax.optimization_barrier((flat_tiles, moved))
    tiles_own = jnp.stack([flat_tiles, swap_x(flat_tiles)])
    tiles_near = swap_core(tiles_own)
    columns_own = jnp.stack([moved, swap_x(moved)])
    columns_near = swap_core(columns_own)
    places = places[:, 0, 0 : 2 * held].reshape(blocks, group, 2 * held)
    rows_all = lax.dynamic_index_in_dim(places, block, 0, keepdims=False)[:, 0:held]
    cols_here = lax.dynamic_index_in_dim(places, held + block, 2, keepdims=False)

    packed = pltpu.VMEM((width, 2 * width), BF16)
    work = pltpu.VMEM((width, 2 * width), F32)
    spread = pltpu.VMEM((2, 8, 8, 2 * width), F32)
    slot_scratch = [pltpu.SMEM((blocks, group), jnp.int32), pltpu.SMEM((share * group // tile,), jnp.int32)]
    for iteration in range(ITERS):
        first, last = iteration == 0, iteration == ITERS - 1
        chosen = across(chosen)
        outs = [shape((blocks, packed_rows, tile), BF16)]
        if last:
            outs.append(shape((width, ROW_TILES * tile), F32))
        results = call(
            functools.partial(left_kernel, first, last),
            outs,
            [],
            [],
            [rows_all, tiles_own, tiles_near, chosen, swap_core(chosen)],
            [
                pltpu.VMEM((width, ROW_TILES * tile), F32),
                pltpu.VMEM((2 * width if first else width, ROW_TILES * tile), BF16),
                packed,
                work,
                spread,
                pltpu.VMEM((width, 2 * width), F32),
                pltpu.SMEM(rows_all.shape, jnp.int32),
                pltpu.SemaphoreType.DMA((1,)),
            ]
            + ([pltpu.SemaphoreType.DMA((blocks, 3))] if first else [])
            + ([pltpu.VMEM((group, blocks, width, tile), F32)] if first and blocks <= 8 else []),
            [HBM] if first else None,
        )
        picked = across(results[0])
        left_raw = results[-1]
        total = pltpu.VMEM((width, count * tile), F32)
        gram_scratch = pltpu.VMEM((width, 2 * width), F32)
        quarters = pltpu.VMEM((group, count, quarter, tile), BF16)
        other = swap_core(picked)
        if last:
            break
        (chosen,) = call(
            right_kernel,
            [shape((blocks, packed_rows, tile), BF16)],
            [],
            [],
            [cols_here, columns_own, columns_near, picked, other],
            [total, pltpu.VMEM((width, count * tile), BF16), packed, work, spread, gram_scratch, quarters]
            + [pltpu.SMEM(cols_here.shape, jnp.int32), pltpu.SemaphoreType.DMA((1,))]
            + slot_scratch,
        )
    (slots,) = call(
        slots_kernel,
        [shape(cols_here.shape, jnp.int32)],
        [cols_here],
        [],
        [],
        slot_scratch[1:],
        [SMEM],
    )
    (gram,) = call(
        last_right_kernel,
        [shape((blocks, width // 2, 2 * width), F32)],
        [],
        [],
        [slots, columns_own, columns_near, picked, other],
        [total, gram_scratch, quarters, pltpu.SMEM(slots.shape, jnp.int32), pltpu.SemaphoreType.DMA((blocks + 1,))],
        [HBM],
    )
    left, parts, left_scale = call(
        functools.partial(between_kernel, math.sqrt(total_rows), math.sqrt(total_cols)),
        [shape(left_raw.shape, F32), shape((2 * width, share), BF16), shape((width, width), F32)],
        [cols_here, slots],
        [],
        [columns_own, columns_near, picked, other, left_raw],
        [pltpu.VMEM((width, share), F32), work, spread, total, gram_scratch, quarters],
    )
    (right,) = call(
        finish_kernel,
        [shape((width, share), F32)],
        [],
        [],
        [across(gram), left_scale, parts],
        [work, spread, pltpu.VMEM((width, share), F32), pltpu.SemaphoreType.DMA((8,))],
        [HBM],
    )
    return (left.T, right.T)


def solution(mesh):
    in_specs = (
        P("blk", "rep", None, None),
        P("blk", "rep"),
        P("blk", "rep"),
        P(("blk", "rep"), None),
    )
    out_specs = (P("blk", None), P(("blk", "rep"), None))
    return jax.shard_map(local, mesh=mesh, in_specs=in_specs, out_specs=out_specs, check_vma=False)
```
